128 devices in a mesh: lat: 16 (over x, z_hi, core), lon: 8 (over z_lo, y).
Axes of the slice: x: 4, y: 4, z: 4 (z_hi: 2, z_lo: 2; z = z_hi * 2 + z_lo), core: 2. Of those that a mesh axis runs over, the one named last changes fastest.
Arguments:
- fields: bfloat16 [3, 64, 128, 512], P(None, 'lat', 'lon'), may hold values from -6 to 6
- land_sea: int32 [64, 128], P('lat', 'lon'), may hold values 0 or 1
- surface_embed: bfloat16 [2, 512], replicated, may hold values from -4 to 4
- norm_gains: float32 [2, 512], replicated, may hold values from 0.1 to 1.9
- w_qkv: bfloat16 [512, 1536], replicated, may hold values from -0.25 to 0.25
- head_scales: float32 [8], replicated, may hold values from 2 to 20
- w_out: bfloat16 [512, 512], replicated, may hold values from -0.25 to 0.25
- w_up: bfloat16 [512, 2048], replicated, may hold values from -0.25 to 0.25
- w_down: bfloat16 [2048, 512], replicated, may hold values from -0.125 to 0.125
- cotangent: bfloat16 [3, 64, 128, 512], P(None, 'lat', 'lon'), may hold values from -6 to 6
Outputs:
- layer_out: bfloat16 [3, 64, 128, 512], P(None, 'lat', 'lon')
- grad_fields: bfloat16 [3, 64, 128, 512], P(None, 'lat', 'lon')
- grad_qkv: float32 [512, 1536], P(('lat', 'lon'))
- grad_out: float32 [512, 512], P(('lat', 'lon'))
- grad_up: float32 [512, 2048], P(('lat', 'lon'))
- grad_down: float32 [2048, 512], P(('lat', 'lon'))
- grad_gains: float32 [2, 512], P(None, ('lat', 'lon'))
The draws below stay inside these ranges and needn't reach their ends.
Inputs may be any that keep to these rules, and one draw needn't show every extreme that they name: `land_sea`: 1 marks land, 0 sea.
All inputs are finite; a program needn't handle non-finite values. No bound on the sum of `land_sea` on one device may be relied on, other than what follows from the above.
Results may differ from the reference program's by a relative error of at most 0.025.
Values may be sent and summed in bfloat16 or wider, within the bound.
No kernel may reach another device: no remote copies, remote signals or barrier semaphores. Data moves between devices by JAX's collectives and lax.ppermute only.
A program may use at most 128 MiB of HBM per device.

```python
import math
from functools import partial
import jax
import jax.numpy as jnp
from jax import lax

D = 512
HEADS = 8
HEAD_DIM = 64
FF = 2048
WL = 4
SHIFT = 2
LEV = 3
LAT = 64
LON = 128
TOKENS = 24576


def plant(result, own_key, least, largest):
    spot = [jax.random.randint(jax.random.fold_in(own_key, axis), (), 0, length) for axis, length in enumerate(result.shape)]
    widest = result.shape.index(max(result.shape))
    next_to = spot[:widest] + [(spot[widest] + 1) % result.shape[widest]] + spot[widest + 1:]
    return result.at[tuple(spot)].set(least).at[tuple(next_to)].set(largest)


def block_levels(key, dims, pieces, least, high):
    def one(position, parts):
        draws = jax.random.uniform(jax.random.fold_in(jax.random.fold_in(key, 6), position), (parts,), jnp.float32, least / len(pieces), high / len(pieces))
        return jnp.repeat(jnp.exp(draws), dims[position] // parts).reshape((-1,) + (1,) * (len(dims) - position - 1))

    factor_of = one(*pieces[0])
    for cut in pieces[1:]:
        factor_of = factor_of * one(*cut)
    return factor_of


def scatter_about(key, shape, spread, bound, cuts=(), kind=jnp.bfloat16):
    array = spread * jax.random.normal(key, shape, jnp.float32)
    if cuts:
        array = array * block_levels(key, shape, cuts, -0.22, 0.18)
    return jnp.clip(array, -bound, bound).astype(kind)


def setup_inputs(seed: int = 0) -> dict:
    arg_keys = jax.random.split(jax.random.key(seed), 11)
    fields = scatter_about(arg_keys[0], (LEV, LAT, LON, D), 1.0, 6.0, ((1, 16), (2, 8)))
    land_sea = plant((jax.random.randint(arg_keys[1], (LAT, LON), 0, 10) < 3).astype(jnp.int32), jax.random.fold_in(arg_keys[1], 1), 0, 1)
    surface_embed = scatter_about(arg_keys[2], (2, D), 1.0, 4.0)
    norm_gains = jnp.clip(1.0 + 0.18 * jax.random.normal(arg_keys[3], (2, D), jnp.float32), 0.1, 1.9)
    w_qkv = scatter_about(arg_keys[4], (D, 3 * D), D ** -0.5, 0.25)
    head_scales = jnp.clip(jnp.exp(jax.random.uniform(arg_keys[5], (HEADS,), jnp.float32, math.log(2.0), math.log(20.0))), 2.0, 20.0)
    w_out = scatter_about(arg_keys[6], (D, D), D ** -0.5, 0.25)
    w_up = scatter_about(arg_keys[7], (D, FF), D ** -0.5, 0.25)
    w_down = scatter_about(arg_keys[8], (FF, D), FF ** -0.5, 0.125)
    cotangent = scatter_about(arg_keys[9], (LEV, LAT, LON, D), 1.0, 6.0, ((1, 16), (2, 8)))
    return {"fields": fields, "land_sea": land_sea, "surface_embed": surface_embed, "norm_gains": norm_gains, "w_qkv": w_qkv, "head_scales": head_scales, "w_out": w_out, "w_up": w_up, "w_down": w_down, "cotangent": cotangent}


def layer_norm(values, gain_row):
    row_mean = lax.optimization_barrier(jnp.mean(values, axis=-1, keepdims=True))
    centred = values - row_mean
    variance = lax.optimization_barrier(jnp.mean(centred * centred, axis=-1, keepdims=True))
    return centred * lax.rsqrt(variance + 1e-05) * gain_row

def unit_heads(values, head_count):
    shaped = values.reshape(values.shape[:-1] + (head_count, values.shape[-1] // head_count))
    scaled = shaped * lax.rsqrt(lax.optimization_barrier(jnp.sum(shaped * shaped, axis=-1, keepdims=True)) + 1e-06)
    return scaled.reshape(values.shape)

def attend(query_block, key_block, value_block, key_valid, head_scales):
    scores = jnp.einsum('qhe,khe->hqk', query_block.astype(jnp.float32), key_block.astype(jnp.float32)) * head_scales[:, None, None]
    exp_scores = jnp.exp(scores) * key_valid[None, None, :]
    inverse = 1.0 / lax.optimization_barrier(jnp.sum(exp_scores, axis=2))
    attn_probs = (exp_scores * inverse[:, :, None]).astype(jnp.bfloat16)
    attended = jnp.einsum('hqk,khe->qhe', attn_probs.astype(jnp.float32), value_block.astype(jnp.float32)).astype(jnp.bfloat16)
    return (attended, attn_probs)

def attend_back(query_block, key_block, value_block, key_valid, attended, grad_block, head_scales):
    attn_probs = attend(query_block, key_block, value_block, key_valid, head_scales)[1]
    row_delta = lax.optimization_barrier(jnp.sum(grad_block.astype(jnp.float32) * attended.astype(jnp.float32), axis=2)).T
    grad_probs = jnp.einsum('qhe,khe->hqk', grad_block.astype(jnp.float32), value_block.astype(jnp.float32))
    grad_scores = (attn_probs.astype(jnp.float32) * (grad_probs - row_delta[:, :, None]) * head_scales[:, None, None]).astype(jnp.bfloat16)
    grad_query = jnp.einsum('hqk,khe->qhe', grad_scores.astype(jnp.float32), key_block.astype(jnp.float32))
    grad_key = jnp.einsum('hqk,qhe->khe', grad_scores.astype(jnp.float32), query_block.astype(jnp.float32))
    grad_value = jnp.einsum('hqk,qhe->khe', attn_probs.astype(jnp.float32), grad_block.astype(jnp.float32))
    return (grad_query, grad_key, grad_value)

def to_windows(grid_rows):
    grid = grid_rows.reshape(LEV, LAT, LON, D)
    padded = jnp.pad(grid, ((0, 0), (SHIFT, SHIFT), (0, 0), (0, 0)))
    window_count = (LAT + 2 * SHIFT) // WL
    shaped = padded.reshape(LEV, window_count, WL, LON, HEADS, HEAD_DIM)
    return jnp.moveaxis(shaped, 1, 0).reshape(window_count, LEV * WL * LON, HEADS, HEAD_DIM)

def from_windows(blocks):
    window_count = blocks.shape[0]
    shaped = jnp.moveaxis(blocks.reshape(window_count, LEV, WL, LON, HEADS, HEAD_DIM), 0, 1)
    return shaped.reshape(LEV, window_count * WL, LON, D)[:, SHIFT:SHIFT + LAT].reshape(-1, D)

def reference(fields, land_sea, surface_embed, norm_gains, w_qkv, head_scales, w_out, w_up, w_down, cotangent):
    chosen = jnp.where(land_sea[None, :, :, None] == 1, surface_embed[1].astype(jnp.float32), surface_embed[0].astype(jnp.float32))
    hidden = (fields.astype(jnp.float32) + chosen).astype(jnp.bfloat16)
    hidden_wide = hidden.reshape(-1, D).astype(jnp.float32)
    normed_wide, norm_back_one = jax.vjp(layer_norm, hidden_wide, norm_gains[0])
    normed = normed_wide.astype(jnp.bfloat16)
    projected = jnp.dot(normed, w_qkv, preferred_element_type=jnp.float32)
    unit_fn = partial(unit_heads, head_count=HEADS)
    query_wide, query_back = jax.vjp(unit_fn, projected[:, :D])
    key_wide, key_back = jax.vjp(unit_fn, projected[:, D:2 * D])
    query_unit = query_wide.astype(jnp.bfloat16)
    key_unit = key_wide.astype(jnp.bfloat16)
    value_rows = projected[:, 2 * D:].astype(jnp.bfloat16)
    window_count = (LAT + 2 * SHIFT) // WL
    row_index = jnp.arange(LAT + 2 * SHIFT, dtype=jnp.int32)
    row_valid = ((row_index >= SHIFT) & (row_index < SHIFT + LAT)).astype(jnp.float32)
    key_valid = jnp.broadcast_to(row_valid.reshape(window_count, 1, WL, 1), (window_count, LEV, WL, LON)).reshape(window_count, -1)
    query_win = to_windows(query_unit)
    key_win = to_windows(key_unit)
    value_win = to_windows(value_rows)

    def forward_window(block):
        return attend(block[0], block[1], block[2], block[3], head_scales)[0]
    attended_win = lax.map(forward_window, (query_win, key_win, value_win, key_valid))
    attended = from_windows(attended_win)
    mixed = (hidden_wide + jnp.dot(attended, w_out, preferred_element_type=jnp.float32)).astype(jnp.bfloat16)
    mixed_wide = mixed.astype(jnp.float32)
    normed_two_wide, norm_back_two = jax.vjp(layer_norm, mixed_wide, norm_gains[1])
    normed_two = normed_two_wide.astype(jnp.bfloat16)
    pre_act = jnp.dot(normed_two, w_up, preferred_element_type=jnp.float32)
    act_wide, gelu_back = jax.vjp(jax.nn.gelu, pre_act)
    activated = act_wide.astype(jnp.bfloat16)
    layer_out = (mixed_wide + jnp.dot(activated, w_down, preferred_element_type=jnp.float32)).astype(jnp.bfloat16)
    grad_rows = cotangent.reshape(-1, D)
    grad_act = jnp.dot(grad_rows, w_down.T, preferred_element_type=jnp.float32)
    grad_pre = gelu_back(grad_act)[0].astype(jnp.bfloat16)
    grad_normed_two = jnp.dot(grad_pre, w_up.T, preferred_element_type=jnp.float32)
    grad_mixed_part, grad_gain_two = norm_back_two(grad_normed_two)
    grad_mixed = grad_rows.astype(jnp.float32) + grad_mixed_part
    grad_mixed_low = grad_mixed.astype(jnp.bfloat16)
    grad_attended = jnp.dot(grad_mixed_low, w_out.T, preferred_element_type=jnp.float32).astype(jnp.bfloat16)
    grad_win = to_windows(grad_attended)

    def backward_window(block):
        return attend_back(block[0], block[1], block[2], block[3], block[4], block[5], head_scales)
    grad_query_win, grad_key_win, grad_value_win = lax.map(backward_window, (query_win, key_win, value_win, key_valid, attended_win, grad_win))
    grad_query = from_windows(grad_query_win)
    grad_key = from_windows(grad_key_win)
    grad_value = from_windows(grad_value_win)
    grad_projected = jnp.concatenate([query_back(grad_query)[0], key_back(grad_key)[0], grad_value], axis=1).astype(jnp.bfloat16)
    grad_normed = jnp.dot(grad_projected, w_qkv.T, preferred_element_type=jnp.float32)
    grad_hidden_part, grad_gain_one = norm_back_one(grad_normed)
    grad_fields = (grad_mixed + grad_hidden_part).astype(jnp.bfloat16).reshape(fields.shape)
    grad_scale = 1.0 / math.sqrt(TOKENS)
    grad_qkv = jnp.dot(normed.T, grad_projected, preferred_element_type=jnp.float32) * grad_scale
    grad_out = jnp.dot(attended.T, grad_mixed_low, preferred_element_type=jnp.float32) * grad_scale
    grad_up = jnp.dot(normed_two.T, grad_pre, preferred_element_type=jnp.float32) * grad_scale
    grad_down = jnp.dot(activated.T, grad_rows, preferred_element_type=jnp.float32) * grad_scale
    grad_gains = jnp.stack([grad_gain_one, grad_gain_two]) * grad_scale
    return (layer_out.reshape(fields.shape), grad_fields, grad_qkv, grad_out, grad_up, grad_down, grad_gains)
```

```python
import math

import jax
import jax.numpy as jnp
from jax import lax
from jax.experimental import pallas as pl
from jax.experimental.pallas import tpu as pltpu
from jax.sharding import Mesh
from jax.sharding import PartitionSpec as P

LAT = ("x", "zh", "c")
LON = ("zl", "y")
ALL = LAT + LON
AXIS_SIZES = (4, 2, 2, 2, 4)

HEADS = 8
HEAD = 64
D = 512
FF = 2048
HALF = 96
ROWS = 768
OWN = 2 * HALF
QT = 256

F32 = jnp.float32
BF16 = jnp.bfloat16
NT = (((1,), (1,)), ((), ()))
TN = (((0,), (0,)), ((), ()))


def dot(a, b):
    return jnp.dot(a, b, preferred_element_type=F32)


def dot_nt(a, b):
    return lax.dot_general(a, b, NT, preferred_element_type=F32)


def dot_tn(a, b):
    return lax.dot_general(a, b, TN, preferred_element_type=F32)


def norm_stats(values):
    centred = values - jnp.mean(values, axis=-1, keepdims=True)
    variance = jnp.mean(centred * centred, axis=-1, keepdims=True)
    inverse = lax.rsqrt(variance + 1e-05)
    return centred * inverse, inverse


def norm_back(grad, unit, inverse, gain):
    scaled = grad * gain
    first = jnp.mean(scaled, axis=-1, keepdims=True)
    second = jnp.mean(scaled * unit, axis=-1, keepdims=True)
    return inverse * (scaled - first - unit * second)


def unit_rows(values):
    inverse = lax.rsqrt(jnp.sum(values * values, axis=-1, keepdims=True) + 1e-06)
    return values * inverse, inverse


def unit_back(grad, unit, inverse):
    return inverse * (grad - unit * jnp.sum(grad * unit, axis=-1, keepdims=True))


def pack_head(array, column):
    cols = slice(column, column + HEAD)
    return [array[:HALF, cols], array[HALF:, cols]]


def unpack_heads(ref, lane):
    return jnp.concatenate([ref[h, :, lane : lane + HEAD] for h in range(HEADS)], axis=1)


def project_kernel(low_ref, up_ref, gain_ref, w_ref, normed_ref, packed_ref):
    hidden = jnp.concatenate([low_ref[...], up_ref[...]], axis=0).astype(F32)
    unit, _ = norm_stats(hidden)
    normed = (unit * gain_ref[0:1, :]).astype(BF16)
    normed_ref[0] = normed[:HALF]
    normed_ref[1] = normed[HALF:]
    projected = dot(normed, w_ref[...]).astype(BF16)
    for h in range(HEADS):
        pieces = []
        for part in range(3):
            pieces += pack_head(projected, part * D + h * HEAD)
        packed_ref[h] = jnp.concatenate(pieces, axis=1)


def load_heads(x_ref, offset, half):
    start = offset + half * HEAD
    return x_ref[:, start : start + HEAD]


def lane_ones(count):
    lanes = lax.broadcasted_iota(jnp.int32, (ROWS, HEAD), 1)
    return jnp.where(lanes < count, 1.0, 0.0).astype(BF16)


def attend_kernel(scal_ref, x_ref, att_ref, inv_ref, q_s, k_s, v_s):
    factor = scal_ref[0]
    other = scal_ref[2].astype(BF16)
    for a in range(2):
        rows = slice(a * ROWS, (a + 1) * ROWS)
        q_s[rows] = unit_rows(load_heads(x_ref, 0, a).astype(F32))[0].astype(BF16)
        k_s[rows] = unit_rows(load_heads(x_ref, 128, a).astype(F32))[0].astype(BF16)
        wide = jnp.concatenate([load_heads(x_ref, 256, a), lane_ones(1)], axis=1)
        v_s[a, rows] = wide
        v_s[1 - a, rows] = wide * other
    for t in range(2 * ROWS // QT):
        rows = slice(t * QT, (t + 1) * QT)
        a, inner = divmod(t * QT, ROWS)
        weights = jnp.exp2(dot_nt(q_s[rows], k_s[...]) * factor).astype(BF16)
        total = dot(weights, v_s[a])
        inverse = 1.0 / total[:, HEAD : HEAD + 1]
        inv_ref[rows] = inverse
        att_ref[inner : inner + QT, a * HEAD : (a + 1) * HEAD] = (
            total[:, :HEAD] * inverse
        ).astype(BF16)


def attend_back_kernel(
    scal_ref, x_ref, grad_ref, att_ref, inv_ref, normed_ref, out_ref, gw_ref,
    q_s, k_s, kt_s, v_s, g_s, gv_s, dq_s, dk_s, dv_s,
):
    factor = scal_ref[0]
    scale = scal_ref[1]
    other = scal_ref[2].astype(BF16)
    for a in range(2):
        rows = slice(a * ROWS, (a + 1) * ROWS)
        q_s[rows] = unit_rows(load_heads(x_ref, 0, a).astype(F32))[0].astype(BF16)
        key_unit = unit_rows(load_heads(x_ref, 128, a).astype(F32))[0].astype(BF16)
        k_s[rows] = key_unit
        kt_s[:, rows] = key_unit.astype(F32).T.astype(BF16)
        wide = jnp.concatenate([load_heads(x_ref, 256, a), lane_ones(2)], axis=1)
        v_s[a, rows] = wide
        v_s[1 - a, rows] = wide * other
        grad = load_heads(grad_ref, 0, a).astype(F32)
        inverse = inv_ref[rows]
        delta = jnp.sum(grad * load_heads(att_ref, 0, a).astype(F32), axis=-1, keepdims=True)
        delta = delta * inverse
        delta_high = delta.astype(BF16)
        delta_low = (delta - delta_high.astype(F32)).astype(BF16)
        grad_low = (grad * inverse).astype(BF16)
        lanes = lax.broadcasted_iota(jnp.int32, (ROWS, HEAD), 1)
        tail = jnp.where(
            lanes == 0,
            -delta_high.astype(F32),
            jnp.where(lanes == 1, -delta_low.astype(F32), 0.0),
        ).astype(BF16)
        g_s[rows] = jnp.concatenate([grad_low, tail], axis=1)
        gv_s[0, rows] = grad_low
        gv_s[1, rows] = grad_low * other
    dk_s[...] = jnp.zeros_like(dk_s)
    dv_s[...] = jnp.zeros_like(dv_s)
    for t in range(2 * ROWS // QT):
        rows = slice(t * QT, (t + 1) * QT)
        a = t * QT // ROWS
        query = q_s[rows]
        weights = jnp.exp2(dot_nt(k_s[...], query) * factor)
        grad_weights = dot_nt(v_s[a], g_s[rows])
        grad_scores = (weights * grad_weights).astype(BF16)
        weights = weights.astype(BF16)
        for b in range(2):
            keys = slice(b * ROWS, (b + 1) * ROWS)
            dv_s[keys] += dot(weights[keys], gv_s[abs(a - b), rows])
        dk_s[...] += dot(grad_scores, query)
        dq_s[rows] = dot(kt_s[...], grad_scores).T
    part = None
    for a in range(2):
        rows = slice(a * ROWS, (a + 1) * ROWS)
        unit, inverse = unit_rows(load_heads(x_ref, 0, a).astype(F32))
        dq = unit_back(dq_s[rows] * scale, unit, inverse).astype(BF16)
        unit, inverse = unit_rows(load_heads(x_ref, 128, a).astype(F32))
        dk = unit_back(dk_s[rows] * scale, unit, inverse).astype(BF16)
        dv = dv_s[rows].astype(BF16)
        for place, piece in enumerate((dq, dk, dv)):
            start = place * 128 + a * HEAD
            out_ref[:, start : start + HEAD] = piece
        grads = jnp.concatenate([dq, dk, dv], axis=1)
        normed = jnp.concatenate([normed_ref[i, a] for i in range(8)], axis=0)
        term = dot_tn(normed, grads)
        part = term if part is None else part + term
    gw_ref[...] = part.astype(BF16)


def middle_kernel(
    core_ref, att_ref, low_ref, up_ref, clow_ref, cup_ref, gain_ref, w_out_ref, w_up_ref,
    w_down_ref, out_low_ref, out_up_ref, packed_ref, gm_ref, mine_ref, other_ref,
):
    attended = jnp.concatenate([unpack_heads(att_ref, 0), unpack_heads(att_ref, HEAD)], axis=0)
    hidden = jnp.concatenate([low_ref[...], up_ref[...]], axis=0).astype(F32)
    cot = jnp.concatenate([clow_ref[...], cup_ref[...]], axis=0)
    gain = gain_ref[1:2, :]
    mixed = (hidden + dot(attended, w_out_ref[...])).astype(BF16).astype(F32)
    unit, inverse = norm_stats(mixed)
    normed = (unit * gain).astype(BF16)
    pre = dot(normed, w_up_ref[...])
    root = math.sqrt(2.0 / math.pi)
    square = pre * pre
    bend = jnp.tanh(root * pre * (1.0 + 0.044715 * square))
    half_up = 0.5 * (1.0 + bend)
    activated = (pre * half_up).astype(BF16)
    slope = half_up + 0.5 * pre * (1.0 - bend * bend) * root * (1.0 + 3 * 0.044715 * square)
    layer_out = (mixed + dot(activated, w_down_ref[...])).astype(BF16)
    out_low_ref[...] = layer_out[:HALF]
    out_up_ref[...] = layer_out[HALF:]
    grad_pre = (dot_nt(cot, w_down_ref[...]) * slope).astype(BF16)
    grad_normed = dot_nt(grad_pre, w_up_ref[...])
    grad_mixed = cot.astype(F32) + norm_back(grad_normed, unit, inverse, gain)
    gm_ref[...] = grad_mixed
    grad_low = grad_mixed.astype(BF16)
    grad_attended = dot_nt(grad_low, w_out_ref[...]).astype(BF16)
    for h in range(HEADS):
        packed_ref[h] = jnp.concatenate(pack_head(grad_attended, h * HEAD), axis=1)
    first = core_ref[0] == 0

    def put(product, start, width, step, blocks):
        for g in range(8):
            at = g * 2 * step
            zero = product[at : at + step]
            one = product[at + step : at + 2 * step]
            mine = jnp.where(first, zero, one).astype(BF16)
            other = jnp.where(first, one, zero).astype(BF16)
            for s in range(blocks):
                rows = slice(s * 32, (s + 1) * 32)
                cols = slice(start + s * width, start + (s + 1) * width)
                mine_ref[g, :, cols] = mine[rows]
                other_ref[g, :, cols] = other[rows]

    put(dot_tn(attended, grad_low), 0, D, 32, 1)
    put(dot_tn(normed, grad_pre), D, FF, 32, 1)
    put(dot_tn(activated, cot), D + FF, D, 128, 4)


def input_grad_kernel(packed_ref, low_ref, up_ref, gain_ref, gm_ref, w_ref, glow_ref, gup_ref):
    halves = []
    for a in range(2):
        parts = [unpack_heads(packed_ref, place * 128 + a * HEAD) for place in range(3)]
        halves.append(jnp.concatenate(parts, axis=1))
    grad_projected = jnp.concatenate(halves, axis=0)
    grad_normed = dot_nt(grad_projected, w_ref[...])
    hidden = jnp.concatenate([low_ref[...], up_ref[...]], axis=0).astype(F32)
    unit, inverse = norm_stats(hidden)
    grad = gm_ref[...] + norm_back(grad_normed, unit, inverse, gain_ref[0:1, :])
    grad = grad.astype(BF16)
    glow_ref[...] = grad[:HALF]
    gup_ref[...] = grad[HALF:]


VMEM = pl.BlockSpec(memory_space=pltpu.VMEM)
SMEM = pl.BlockSpec(memory_space=pltpu.SMEM)


def call(kernel, outs, specs, scratch=(), flops=0):
    shapes = tuple(jax.ShapeDtypeStruct(shape, dtype) for shape, dtype in outs)
    return pl.pallas_call(
        kernel,
        out_shape=shapes,
        in_specs=specs,
        out_specs=tuple(VMEM for _ in outs),
        scratch_shapes=list(scratch),
        compiler_params=pltpu.CompilerParams(vmem_limit_bytes=52 * 1024 * 1024),
        cost_estimate=pl.CostEstimate(flops=flops, bytes_accessed=8_000_000, transcendentals=0),
    )


def shards(
    fields, land_sea, surface_embed, norm_gains, w_qkv, head_scales, w_out, w_up, w_down, cotangent
):
    lat = lax.axis_index(LAT)
    lon = lax.axis_index(LON)
    device = lax.axis_index(ALL)
    forward = [(i, (i + 1) % 16) for i in range(16)]
    backward = [(j, i) for i, j in forward]
    chosen = jnp.where(
        land_sea[None, :, :, None] == 1,
        surface_embed[1].astype(F32),
        surface_embed[0].astype(F32),
    )
    hidden = (fields.astype(F32) + chosen).astype(BF16)
    low = lax.ppermute(hidden[:, 2:].reshape(HALF, D), LAT, forward)
    up = hidden[:, :2].reshape(HALF, D)
    cot_low = lax.ppermute(cotangent[:, 2:].reshape(HALF, D), LAT, forward)
    cot_up = cotangent[:, :2].reshape(HALF, D)

    scale = head_scales[lon]
    valid = jnp.where(lat == 0, 0.0, 1.0)
    scal = jnp.stack([scale * math.log2(math.e), scale, valid]).astype(F32)

    normed, packed = call(
        project_kernel,
        [((2, HALF, D), BF16), ((HEADS, HALF, 384), BF16)],
        [VMEM] * 4,
        flops=2 * OWN * D * 3 * D,
    )(low, up, norm_gains, w_qkv)
    normed_all = lax.all_gather(normed, LON, axis=0, tiled=False)
    heads = lax.all_to_all(packed, LON, 0, 0, tiled=True).reshape(ROWS, 384)

    wide = 2 * ROWS
    att, inv = call(
        attend_kernel,
        [((ROWS, 128), BF16), ((wide, 1), F32)],
        [SMEM, VMEM],
        [
            pltpu.VMEM((wide, HEAD), BF16),
            pltpu.VMEM((wide, HEAD), BF16),
            pltpu.VMEM((2, wide, 128), BF16),
        ],
        flops=4 * wide * wide * HEAD,
    )(scal, heads)
    att_rows = lax.all_to_all(att.reshape(HEADS, HALF, 128), LON, 0, 0, tiled=True)

    core = lax.axis_index("c").astype(jnp.int32).reshape(1)
    out_low, out_up, packed_grad, grad_mixed, mine, other = call(
        middle_kernel,
        [
            ((HALF, D), BF16),
            ((HALF, D), BF16),
            ((HEADS, HALF, 128), BF16),
            ((OWN, D), F32),
            ((8, 32, 9 * D), BF16),
            ((8, 32, 9 * D), BF16),
        ],
        [SMEM] + [VMEM] * 9,
        flops=6 * OWN * D * (2 * FF + D),
    )(core, att_rows, low, up, cot_low, cot_up, norm_gains, w_out, w_up, w_down)
    theirs = lax.ppermute(other, "c", [(0, 1), (1, 0)])
    out_back = lax.ppermute(out_low, LAT, backward)
    grad_heads = lax.all_to_all(packed_grad, LON, 0, 0, tiled=True).reshape(ROWS, 128)
    pair = (mine.astype(F32) + theirs.astype(F32)).astype(BF16)
    part = lax.psum_scatter(pair, "x", scatter_dimension=0, tiled=True)

    packed_back, part_qkv = call(
        attend_back_kernel,
        [((ROWS, 384), BF16), ((D, 192), BF16)],
        [SMEM] + [VMEM] * 5,
        [
            pltpu.VMEM((wide, HEAD), BF16),
            pltpu.VMEM((wide, HEAD), BF16),
            pltpu.VMEM((HEAD, wide), BF16),
            pltpu.VMEM((2, wide, 128), BF16),
            pltpu.VMEM((wide, 128), BF16),
            pltpu.VMEM((2, wide, HEAD), BF16),
            pltpu.VMEM((wide, HEAD), F32),
            pltpu.VMEM((wide, HEAD), F32),
            pltpu.VMEM((wide, HEAD), F32),
        ],
        flops=10 * wide * wide * HEAD,
    )(scal, heads, grad_heads, att, inv, normed_all)
    grad_packed = lax.all_to_all(
        packed_back.reshape(HEADS, HALF, 384), LON, 0, 0, tiled=True
    )
    grad_low, grad_up = call(
        input_grad_kernel,
        [((HALF, D), BF16), ((HALF, D), BF16)],
        [VMEM] * 6,
        flops=2 * OWN * D * 3 * D,
    )(grad_packed, low, up, norm_gains, grad_mixed, w_qkv)
    grad_back = lax.ppermute(grad_low, LAT, backward)

    got = lax.all_to_all(part_qkv.reshape(128, 6, 128), ALL, 0, 0, tiled=True)
    got = jnp.sum(got.astype(F32).reshape(16, 8, 6 * 128), axis=0)
    sum_qkv = got.reshape(HEADS, 4, 3, HEAD).transpose(1, 2, 0, 3).reshape(4, 3 * D)
    down_part = part[:, :, 5 * D :].reshape(2, 32, 4, D).transpose(0, 2, 1, 3)
    joined = jnp.concatenate(
        [
            part[:, :, :D].reshape(16, 4 * D),
            part[:, :, D : 5 * D].reshape(16, 4 * FF),
            down_part.reshape(16, 16 * D),
        ],
        axis=1,
    )
    rest = lax.all_to_all(joined.reshape(16, 144, 128), ("zh",) + LON, 0, 0, tiled=True)
    rest = jnp.sum(rest.astype(F32), axis=0).reshape(-1)
    sum_out = rest[: 4 * D].reshape(4, D)
    sum_up = rest[4 * D : 4 * D + 4 * FF].reshape(4, FF)
    sum_down = rest[4 * D + 4 * FF :].reshape(16, D)

    grad_scale = 1.0 / math.sqrt(OWN * 128)
    grad_qkv = sum_qkv * grad_scale
    grad_up_w = sum_up * grad_scale
    rows_qkv = lax.dynamic_slice_in_dim(w_qkv, device * 4, 4, axis=0).astype(F32)
    rows_up = lax.dynamic_slice_in_dim(w_up, device * 4, 4, axis=0).astype(F32)
    gains = lax.dynamic_slice_in_dim(norm_gains, device * 4, 4, axis=1)
    grad_gains = (
        jnp.stack([jnp.sum(rows_qkv * grad_qkv, axis=1), jnp.sum(rows_up * grad_up_w, axis=1)])
        / gains
    )

    def place(own, moved):
        shape = (3, 2, 16, D)
        return jnp.concatenate([own.reshape(shape), moved.reshape(shape)], axis=1)

    return (
        place(out_up, out_back),
        place(grad_up, grad_back),
        grad_qkv,
        sum_out * grad_scale,
        grad_up_w,
        sum_down * grad_scale,
        grad_gains,
    )


def solution(mesh):
    fine = Mesh(mesh.devices.reshape(AXIS_SIZES), ALL)
    grid = P(None, LAT, LON, None)
    in_specs = (grid, P(LAT, LON), P(), P(), P(), P(), P(), P(), P(), grid)
    rows = P(ALL, None)
    out_specs = (grid, grid, rows, rows, rows, rows, P(None, ALL))
    return jax.shard_map(shards, mesh=fine, in_specs=in_specs, out_specs=out_specs, check_vma=False)
```

```python
import math

import jax
import jax.numpy as jnp
from jax import lax
from jax.experimental import pallas as pl
from jax.experimental.pallas import tpu as pltpu
from jax.sharding import Mesh
from jax.sharding import PartitionSpec as P

LAT = ("x", "zh", "c")
LON = ("zl", "y")
ALL = LAT + LON
AXIS_SIZES = (4, 2, 2, 2, 4)

HEADS = 8
HEAD = 64
D = 512
FF = 2048
HALF = 96
ROWS = 768
OWN = 2 * HALF
QT = 256

F32 = jnp.float32
BF16 = jnp.bfloat16
NT = (((1,), (1,)), ((), ()))
TN = (((0,), (0,)), ((), ()))


def dot(a, b):
    return jnp.dot(a, b, preferred_element_type=F32)


def dot_nt(a, b):
    return lax.dot_general(a, b, NT, preferred_element_type=F32)


def dot_tn(a, b):
    return lax.dot_general(a, b, TN, preferred_element_type=F32)


def norm_stats(values):
    centred = values - jnp.mean(values, axis=-1, keepdims=True)
    variance = jnp.mean(centred * centred, axis=-1, keepdims=True)
    inverse = lax.rsqrt(variance + 1e-05)
    return centred * inverse, inverse


def norm_back(grad, unit, inverse, gain):
    scaled = grad * gain
    first = jnp.mean(scaled, axis=-1, keepdims=True)
    second = jnp.mean(scaled * unit, axis=-1, keepdims=True)
    return inverse * (scaled - first - unit * second)


def swap(pair):
    return pltpu.roll(pair, HEAD, axis=1)


def is_left(rows):
    return lax.broadcasted_iota(jnp.int32, (rows, 2 * HEAD), 1) < HEAD


def pair_sum(values):
    row = lax.broadcasted_iota(jnp.int32, (4 * HEAD, 2 * HEAD), 0) >> 6
    column = lax.broadcasted_iota(jnp.int32, (4 * HEAD, 2 * HEAD), 1) >> 6
    ones = jnp.where((row & 1) == column, 1.0, 0.0).astype(BF16)
    high = values.astype(BF16)
    low = (values - high.astype(F32)).astype(BF16)
    return dot(jnp.concatenate([high, low], axis=1), ones)


def unit_pair(x_ref, offset):
    values = x_ref[:, offset : offset + 2 * HEAD].astype(F32)
    inverse = lax.rsqrt(pair_sum(values * values) + 1e-06)
    return values * inverse, inverse


def unit_back(grad, unit, inverse):
    return inverse * (grad - unit * pair_sum(grad * unit))


def spread(pair):
    swapped = swap(pair)
    left = is_left(ROWS)
    return jnp.where(left, pair, swapped), jnp.where(left, swapped, pair)


def put_spread(ref, pair):
    zero, one = spread(pair)
    ref[:ROWS] = zero.astype(BF16)
    ref[ROWS:] = one.astype(BF16)


def pack_head(array, column):
    cols = slice(column, column + HEAD)
    return [array[:HALF, cols], array[HALF:, cols]]


def unpack_heads(ref, lane):
    return jnp.concatenate([ref[h, :, lane : lane + HEAD] for h in range(HEADS)], axis=1)


def project_kernel(low_ref, up_ref, gain_ref, w_ref, normed_ref, packed_ref):
    hidden = jnp.concatenate([low_ref[:HALF], up_ref[...]], axis=0).astype(F32)
    unit, _ = norm_stats(hidden)
    normed = (unit * gain_ref[0:1, :]).astype(BF16)
    normed_ref[0] = normed[:HALF]
    normed_ref[1] = normed[HALF:]
    projected = dot(normed, w_ref[...]).astype(BF16)
    for h in range(HEADS):
        pieces = []
        for part in range(3):
            pieces += pack_head(projected, part * D + h * HEAD)
        packed_ref[h] = jnp.concatenate(pieces, axis=1)


def value_rows(x_ref):
    values = x_ref[:, 4 * HEAD :].astype(F32)
    swapped = swap(values)
    left = is_left(ROWS)
    return [
        [jnp.where(left, values, 1.0), jnp.where(left, swapped, 1.0)],
        [jnp.where(left, 1.0, swapped), jnp.where(left, 1.0, values)],
    ]


def attend_kernel(scal_ref, x_ref, att_ref, inv_ref, q_s, k_s, v_s):
    factor = scal_ref[0]
    other = scal_ref[2]
    put_spread(q_s, unit_pair(x_ref, 0)[0])
    put_spread(k_s, unit_pair(x_ref, 2 * HEAD)[0])
    values = value_rows(x_ref)
    for a in range(2):
        for b in range(2):
            block = values[a][b] if a == b else values[a][b] * other
            v_s[a, b * ROWS : (b + 1) * ROWS] = block.astype(BF16)
    left = is_left(QT)
    for t in range(ROWS // QT):
        totals = []
        for a in range(2):
            start = a * ROWS + t * QT
            scores = dot_nt(q_s[start : start + QT], k_s[...])
            totals.append(dot(jnp.exp2(scores * factor).astype(BF16), v_s[a]))
        inverse = 1.0 / swap(jnp.where(left, totals[1], totals[0]))
        rows = slice(t * QT, (t + 1) * QT)
        inv_ref[rows] = inverse
        att_ref[rows] = (jnp.where(left, totals[0], totals[1]) * inverse).astype(BF16)


def attend_back_kernel(
    scal_ref, core_ref, x_ref, grad_ref, att_ref, inv_ref, normed_ref, out_ref, mine_ref,
    other_ref, q_s, k_s, v_s, g_s, gd_s,
):
    factor = scal_ref[0]
    scale = scal_ref[1]
    other = scal_ref[2]
    left = is_left(ROWS)
    query_unit, query_inverse = unit_pair(x_ref, 0)
    key_unit, key_inverse = unit_pair(x_ref, 2 * HEAD)
    put_spread(q_s, query_unit)
    key_wide = spread(key_unit)
    k_s[:ROWS] = key_wide[0].astype(BF16)
    k_s[ROWS:] = key_wide[1].astype(BF16)
    values = value_rows(x_ref)
    for a in range(2):
        for b in range(2):
            v_s[a, b * ROWS : (b + 1) * ROWS] = values[a][b].astype(BF16)
    grad = grad_ref[...].astype(F32)
    inverse = inv_ref[...]
    delta = swap(pair_sum(grad * att_ref[...].astype(F32)) * inverse)
    high = delta.astype(BF16).astype(F32)
    grad = grad * inverse
    lanes = lax.broadcasted_iota(jnp.int32, (ROWS, 2 * HEAD), 1) & (HEAD - 1)
    tail = jnp.where(lanes == 0, -high, jnp.where(lanes == 1, high - delta, 0.0))
    grad_rows = [jnp.where(left, grad, tail), jnp.where(left, tail, grad)]
    grad_wide = spread(grad)
    for a in range(2):
        rows = slice(a * ROWS, (a + 1) * ROWS)
        for b in range(2):
            mask = 1.0 if a == b else other
            g_s[b, rows] = (grad_rows[a] * mask).astype(BF16)
            gd_s[b, rows] = (grad_wide[a] * mask).astype(BF16)
    dq = [None, None]
    dk = [None, None]
    dv = [None, None]

    def add(sums, place, term):
        sums[place] = term if sums[place] is None else sums[place] + term

    for b in range(2):
        keys = slice(b * ROWS, (b + 1) * ROWS)
        key = k_s[keys]
        key_flat = key_wide[b].T.astype(BF16)
        for a in range(2):
            rows = slice(a * ROWS, (a + 1) * ROWS)
            query = q_s[rows]
            weights = jnp.exp2(dot_nt(key, query) * factor)
            grad_weights = dot_nt(v_s[a, keys], g_s[b, rows])
            grad_scores = (weights * grad_weights).astype(BF16)
            add(dv, b, dot(weights.astype(BF16), gd_s[b, rows]))
            add(dk, b, dot(grad_scores, query))
            add(dq, a, dot(key_flat, grad_scores))
    dq_pair = jnp.where(left, dq[0].T, dq[1].T) * scale
    dk_pair = jnp.where(left, dk[0], dk[1]) * scale
    out_ref[:, : 2 * HEAD] = unit_back(dq_pair, query_unit, query_inverse).astype(BF16)
    out_ref[:, 2 * HEAD : 4 * HEAD] = unit_back(dk_pair, key_unit, key_inverse).astype(BF16)
    out_ref[:, 4 * HEAD :] = jnp.where(left, dv[0], dv[1]).astype(BF16)
    product = None
    for a in range(2):
        pieces = []
        for part in range(3):
            start = part * 2 * HEAD + a * HEAD
            pieces.append(out_ref[:, start : start + HEAD])
        normed = jnp.concatenate([normed_ref[i, a] for i in range(8)], axis=0)
        term = dot_tn(normed, jnp.concatenate(pieces, axis=1))
        product = term if product is None else product + term
    first = core_ref[0] == 0
    for g in range(8):
        zero = product[g * 64 : g * 64 + 32]
        one = product[g * 64 + 32 : g * 64 + 64]
        mine_ref[g] = jnp.where(first, zero, one).astype(BF16)
        other_ref[g] = jnp.where(first, one, zero).astype(BF16)


def pair_kernel(x_ref, mine_ref, theirs_ref, zero_ref, one_ref, two_ref, three_ref):
    for k, ref in enumerate((zero_ref, one_ref, two_ref, three_ref)):
        block = pl.ds(((x_ref[0] + k) & 3) * 2, 2)
        ref[...] = (mine_ref[block].astype(F32) + theirs_ref[block].astype(F32)).astype(BF16)


def join_kernel(part_ref, zero_ref, one_ref, two_ref, three_ref, out_ref):
    for z in range(2):
        narrow = part_ref[z, :, : 5 * D].astype(F32)
        qkv = zero_ref[z].astype(F32)
        for ref in (one_ref, two_ref, three_ref):
            qkv = qkv + ref[z].astype(F32)
        for j in range(8):
            rows = slice(4 * j, 4 * j + 4)
            out_ref[z * 8 + j, :, : 5 * D] = narrow[rows].astype(BF16)
            start = 5 * D + D * (j // 2)
            down = part_ref[z, 16 * (j % 2) : 16 * (j % 2) + 16, start : start + D].astype(F32)
            for s in range(4):
                cols = slice((5 + s) * D, (6 + s) * D)
                out_ref[z * 8 + j, :, cols] = down[4 * s : 4 * s + 4].astype(BF16)
            padded = jnp.concatenate([qkv[rows], jnp.zeros((4, HEAD), F32)], axis=1)
            out_ref[z * 8 + j, :, 9 * D :] = padded.astype(BF16)


def last_kernel(
    got_ref, qkv_rows_ref, up_rows_ref, gains_ref, qkv_ref, out_ref, up_ref, down_ref, gain_ref
):
    grad_scale = 1.0 / math.sqrt(OWN * 128)
    total = got_ref[0, :, : 9 * D].astype(F32)
    for i in range(1, 16):
        total = total + got_ref[i, :, : 9 * D].astype(F32)
    total = total * grad_scale
    out_ref[...] = total[:, :D]
    up = total[:, D : 5 * D]
    up_ref[...] = up
    for s in range(4):
        down_ref[4 * s : 4 * s + 4] = total[:, (5 + s) * D : (6 + s) * D]
    heads = []
    for h in range(HEADS):
        pair = got_ref[h, :, 9 * D :].astype(F32) + got_ref[8 + h, :, 9 * D :].astype(F32)
        heads.append(pair * grad_scale)
    pieces = [heads[h][:, p * HEAD : (p + 1) * HEAD] for p in range(3) for h in range(HEADS)]
    qkv = jnp.concatenate(pieces, axis=1)
    qkv_ref[...] = qkv
    eye = lax.broadcasted_iota(jnp.int32, (4, 4), 0) == lax.broadcasted_iota(
        jnp.int32, (4, 4), 1
    )
    products = (qkv * qkv_rows_ref[...].astype(F32), up * up_rows_ref[...].astype(F32))
    for i, product in enumerate(products):
        column = jnp.sum(product, axis=1, keepdims=True)
        row = jnp.sum(jnp.where(eye, column, 0.0), axis=0, keepdims=True)
        gain_ref[i : i + 1] = row / gains_ref[i : i + 1]


def enter_kernel(
    field_ref, mask_ref, embed_ref, cot_ref, low_ref, up_ref, cup_ref
):
    sea = embed_ref[0:1].astype(F32)
    land = embed_ref[1:2].astype(F32)
    mask = (mask_ref[...] == 1).astype(F32)
    eye = lax.broadcasted_iota(jnp.int32, (16, 16), 0) == lax.broadcasted_iota(
        jnp.int32, (16, 16), 1
    )
    for row in range(4):
        column = jnp.sum(jnp.where(eye, mask[row : row + 1], 0.0), axis=1, keepdims=True)
        chosen = jnp.where(column > 0.5, land, sea)
        hidden_ref, grad_ref = (up_ref, cup_ref) if row < 2 else (low_ref, low_ref)
        offset = 0 if row < 2 else HALF
        for level in range(3):
            start = (level * 2 + row % 2) * 16
            rows = slice(start, start + 16)
            hidden_ref[rows] = (field_ref[level, row].astype(F32) + chosen).astype(BF16)
            grad_ref[offset + start : offset + start + 16] = cot_ref[level, row]


def core_columns(array, width, core):
    pieces = [
        array[:, (2 * g + core) * width : (2 * g + core + 1) * width] for g in range(8)
    ]
    return jnp.concatenate(pieces, axis=1)


def middle_kernel(
    core_ref, att_ref, low_ref, up_ref, cup_ref, gain_ref, w_out_ref, w_up_ref, w_down_ref,
    out_low_ref, out_up_ref, packed_ref, gm_ref, send_ref, keep_ref,
):
    first = core_ref[0] == 0
    attended = jnp.concatenate([unpack_heads(att_ref, 0), unpack_heads(att_ref, HEAD)], axis=0)
    hidden = jnp.concatenate([low_ref[:HALF], up_ref[...]], axis=0).astype(F32)
    cot = jnp.concatenate([low_ref[HALF:], cup_ref[...]], axis=0)
    gain = gain_ref[1:2, :]
    mixed = (hidden + dot(attended, w_out_ref[...])).astype(BF16).astype(F32)
    unit, inverse = norm_stats(mixed)
    normed = (unit * gain).astype(BF16)
    pre = dot(normed, w_up_ref[...])
    root = math.sqrt(2.0 / math.pi)
    square = pre * pre
    bend = jnp.tanh(root * pre * (1.0 + 0.044715 * square))
    half_up = 0.5 * (1.0 + bend)
    activated = (pre * half_up).astype(BF16)
    slope = half_up + 0.5 * pre * (1.0 - bend * bend) * root * (1.0 + 3 * 0.044715 * square)
    grad_pre = (dot_nt(cot, w_down_ref[...]) * slope).astype(BF16)
    grad_normed = dot_nt(grad_pre, w_up_ref[...])
    grad_mixed = cot.astype(F32) + norm_back(grad_normed, unit, inverse, gain)
    gm_ref[...] = grad_mixed
    grad_low = grad_mixed.astype(BF16)
    grad_attended = dot_nt(grad_low, w_out_ref[...]).astype(BF16)
    for h in range(HEADS):
        packed_ref[h] = jnp.concatenate(pack_head(grad_attended, h * HEAD), axis=1)
    layer_out = (mixed + dot(activated, w_down_ref[...])).astype(BF16)
    out_low_ref[...] = layer_out[:HALF]
    out_up_ref[...] = layer_out[HALF:]
    start = 0
    for array, width in ((activated, 128), (normed, 32), (attended, 32)):
        zero = core_columns(array, width, 0)
        one = core_columns(array, width, 1)
        cols = slice(start, start + 8 * width)
        keep_ref[:, cols] = jnp.where(first, zero, one)
        send_ref[:, cols] = jnp.where(first, one, zero)
        start += 8 * width
    for array in (cot, grad_pre, grad_low):
        send_ref[:, start : start + array.shape[1]] = array
        start += array.shape[1]


def partial_kernel(keep_ref, sent_ref, got_ref, out_ref):
    def both(own_ref, start, width):
        cols = slice(start, start + width)
        return jnp.concatenate([own_ref[:, cols], got_ref[:, cols]], axis=0)

    product = dot_tn(both(keep_ref, 0, 2 * D), both(sent_ref, 3 * D, D)).astype(BF16)
    for g in range(8):
        for s in range(4):
            at = g * 128 + s * 32
            out_ref[g, :, (5 + s) * D : (6 + s) * D] = product[at : at + 32]
    product = dot_tn(both(keep_ref, 2 * D, D // 2), both(sent_ref, 4 * D, FF)).astype(BF16)
    for g in range(8):
        out_ref[g, :, D : 5 * D] = product[g * 32 : g * 32 + 32]
    product = dot_tn(both(keep_ref, 5 * D // 2, D // 2), both(sent_ref, 8 * D, D)).astype(BF16)
    for g in range(8):
        out_ref[g, :, :D] = product[g * 32 : g * 32 + 32]


def input_grad_kernel(
    packed_ref, low_ref, up_ref, gain_ref, gm_ref, w_ref, glow_ref, gup_ref
):
    halves = []
    for a in range(2):
        parts = [unpack_heads(packed_ref, place * 128 + a * HEAD) for place in range(3)]
        halves.append(jnp.concatenate(parts, axis=1))
    grad_projected = jnp.concatenate(halves, axis=0)
    hidden = jnp.concatenate([low_ref[:HALF], up_ref[...]], axis=0).astype(F32)
    unit, inverse = norm_stats(hidden)
    grad_normed = dot_nt(grad_projected, w_ref[...])
    grad = gm_ref[...] + norm_back(grad_normed, unit, inverse, gain_ref[0:1, :])
    grad = grad.astype(BF16)
    glow_ref[...] = grad[:HALF]
    gup_ref[...] = grad[HALF:]


VMEM = pl.BlockSpec(memory_space=pltpu.VMEM)
SMEM = pl.BlockSpec(memory_space=pltpu.SMEM)


def call(kernel, outs, specs, scratch=(), vmem=12, cost=0):
    shapes = tuple(jax.ShapeDtypeStruct(shape, dtype) for shape, dtype in outs)
    return pl.pallas_call(
        kernel,
        out_shape=shapes,
        in_specs=specs,
        out_specs=(VMEM,) * len(outs),
        scratch_shapes=list(scratch),
        compiler_params=pltpu.CompilerParams(vmem_limit_bytes=vmem * 1024 * 1024),
        cost_estimate=pl.CostEstimate(flops=0, bytes_accessed=cost, transcendentals=0),
    )


def shards(
    fields, land_sea, surface_embed, norm_gains, w_qkv, head_scales, w_out, w_up, w_down, cotangent
):
    lat = lax.axis_index(LAT)
    lon = lax.axis_index(LON)
    device = lax.axis_index(ALL)
    core = lax.axis_index("c").astype(jnp.int32).reshape(1)
    x_index = lax.axis_index("x").astype(jnp.int32).reshape(1)
    forward = [(i, (i + 1) % 16) for i in range(16)]
    backward = [(j, i) for i, j in forward]
    across = [(0, 1), (1, 0)]
    half = ((HALF, D), BF16)
    low, up, cot_up = call(enter_kernel, [((OWN, D), BF16), half, half], [VMEM] * 4, cost=20_000_000)(
        fields, land_sea, surface_embed, cotangent
    )
    low = lax.ppermute(low, LAT, forward)

    scale = head_scales[lon]
    valid = jnp.where(lat == 0, 0.0, 1.0)
    scal = jnp.stack([scale * (0.5 * math.log2(math.e)), scale, valid]).astype(F32)
    rows_qkv = lax.dynamic_slice_in_dim(w_qkv, device * 4, 4, axis=0)
    rows_up = lax.dynamic_slice_in_dim(w_up, device * 4, 4, axis=0)
    gains = lax.dynamic_slice_in_dim(norm_gains, device * 4, 4, axis=1)
    scal, rows_qkv, rows_up, gains = lax.optimization_barrier((scal, rows_qkv, rows_up, gains))

    normed, packed = call(
        project_kernel,
        [((2, HALF, D), BF16), ((HEADS, HALF, 384), BF16)],
        [VMEM] * 4,
        vmem=12,
        cost=8_000_000,
    )(low, up, norm_gains, w_qkv)
    normed_all = lax.all_gather(normed, LON, axis=0, tiled=False)
    heads = lax.all_to_all(packed, LON, 0, 0, tiled=True).reshape(ROWS, 384)

    wide = 2 * ROWS
    att, inv = call(
        attend_kernel,
        [((ROWS, 128), BF16), ((ROWS, 128), F32)],
        [SMEM, VMEM],
        [
            pltpu.VMEM((wide, 128), BF16),
            pltpu.VMEM((wide, 128), BF16),
            pltpu.VMEM((2, wide, 128), BF16),
        ],
        vmem=20,
        cost=20_000_000,
    )(scal, heads)
    att_rows = lax.all_to_all(att.reshape(HEADS, HALF, 128), LON, 0, 0, tiled=True)

    out_low, out_up, packed_grad, grad_mixed, sent, keep = call(
        middle_kernel,
        [
            half,
            half,
            ((HEADS, HALF, 128), BF16),
            ((OWN, D), F32),
            ((OWN, 9 * D), BF16),
            ((OWN, 3 * D), BF16),
        ],
        [SMEM] + [VMEM] * 8,
        vmem=24,
    )(core, att_rows, low, up, cot_up, norm_gains, w_out, w_up, w_down)
    grad_heads = lax.all_to_all(packed_grad, LON, 0, 0, tiled=True).reshape(ROWS, 128)
    received = lax.ppermute(sent, "c", across)
    out_back = lax.ppermute(out_low, LAT, backward)
    (pair,) = call(partial_kernel, [((8, 32, 9 * D), BF16)], [VMEM] * 3, vmem=24)(
        keep, sent, received
    )
    part = lax.psum_scatter(pair, "x", scatter_dimension=0, tiled=True)

    block = ((8, 32, 192), BF16)
    packed_back, mine, other = call(
        attend_back_kernel,
        [((ROWS, 384), BF16), block, block],
        [SMEM] * 2 + [VMEM] * 5,
        [
            pltpu.VMEM((wide, 128), BF16),
            pltpu.VMEM((wide, 128), BF16),
            pltpu.VMEM((2, wide, 128), BF16),
            pltpu.VMEM((2, wide, 128), BF16),
            pltpu.VMEM((2, wide, 128), BF16),
        ],
        vmem=32,
        cost=1_000_000_000,
    )(scal, core, heads, grad_heads, att, inv, normed_all)
    grad_packed = lax.all_to_all(
        packed_back.reshape(HEADS, HALF, 384), LON, 0, 0, tiled=True
    )
    theirs = lax.ppermute(other, "c", across)
    blocks = call(pair_kernel, [((2, 32, 192), BF16)] * 4, [SMEM, VMEM, VMEM])(
        x_index, mine, theirs
    )
    blocks = [blocks[0]] + [
        lax.ppermute(blocks[k], "x", [(i, (i + k) % 4) for i in range(4)]) for k in (1, 2, 3)
    ]
    grad_low, grad_up = call(
        input_grad_kernel,
        [half] * 2,
        [VMEM] * 6,
        vmem=12,
    )(grad_packed, low, up, norm_gains, grad_mixed, w_qkv)

    part, grad_low, grad_up = lax.optimization_barrier((part, grad_low, grad_up))
    grad_back = lax.ppermute(grad_low, LAT, backward)
    (joined,) = call(join_kernel, [((16, 4, 9 * D + 256), BF16)], [VMEM] * 5)(part, *blocks)
    got = lax.all_to_all(joined, ("zh",) + LON, 0, 0, tiled=True)
    grad_qkv, grad_out, grad_up_w, grad_down, grad_gains = call(
        last_kernel,
        [
            ((4, 3 * D), F32),
            ((4, D), F32),
            ((4, FF), F32),
            ((16, D), F32),
            ((2, 4), F32),
        ],
        [VMEM] * 4,
    )(got, rows_qkv, rows_up, gains)

    def place(own, moved):
        shape = (3, 2, 16, D)
        return jnp.concatenate([own.reshape(shape), moved.reshape(shape)], axis=1)

    return (
        place(out_up, out_back),
        place(grad_up, grad_back),
        grad_qkv,
        grad_out,
        grad_up_w,
        grad_down,
        grad_gains,
    )


def solution(mesh):
    fine = Mesh(mesh.devices.reshape(AXIS_SIZES), ALL)
    grid = P(None, LAT, LON, None)
    in_specs = (grid, P(LAT, LON), P(), P(), P(), P(), P(), P(), P(), grid)
    rows = P(ALL, None)
    out_specs = (grid, grid, rows, rows, rows, rows, P(None, ALL))
    return jax.shard_map(shards, mesh=fine, in_specs=in_specs, out_specs=out_specs, check_vma=False)
```

```python
import math

import jax
import jax.numpy as jnp
from jax import lax
from jax.experimental import pallas as pl
from jax.experimental.pallas import tpu as pltpu
from jax.sharding import Mesh
from jax.sharding import PartitionSpec as P

LAT = ("x", "zh", "c")
LON = ("zl", "y")
ALL = LAT + LON
AXIS_SIZES = (4, 2, 2, 2, 4)

HEADS = 8
HEAD = 64
D = 512
FF = 2048
HALF = 96
ROWS = 768
OWN = 2 * HALF
QT = 256

F32 = jnp.float32
BF16 = jnp.bfloat16
NT = (((1,), (1,)), ((), ()))
TN = (((0,), (0,)), ((), ()))


def dot(a, b):
    return jnp.dot(a, b, preferred_element_type=F32)


def dot_nt(a, b):
    return lax.dot_general(a, b, NT, preferred_element_type=F32)


def dot_tn(a, b):
    return lax.dot_general(a, b, TN, preferred_element_type=F32)


def norm_stats(values):
    centred = values - jnp.mean(values, axis=-1, keepdims=True)
    variance = jnp.mean(centred * centred, axis=-1, keepdims=True)
    inverse = lax.rsqrt(variance + 1e-05)
    return centred * inverse, inverse


def norm_back(grad, unit, inverse, gain):
    scaled = grad * gain
    first = jnp.mean(scaled, axis=-1, keepdims=True)
    second = jnp.mean(scaled * unit, axis=-1, keepdims=True)
    return inverse * (scaled - first - unit * second)


def swap(pair):
    return pltpu.roll(pair, HEAD, axis=1)


def is_left(rows):
    return lax.broadcasted_iota(jnp.int32, (rows, 2 * HEAD), 1) < HEAD


def pair_sum(values):
    row = lax.broadcasted_iota(jnp.int32, (4 * HEAD, 2 * HEAD), 0) >> 6
    column = lax.broadcasted_iota(jnp.int32, (4 * HEAD, 2 * HEAD), 1) >> 6
    ones = jnp.where((row & 1) == column, 1.0, 0.0).astype(BF16)
    high = values.astype(BF16)
    low = (values - high.astype(F32)).astype(BF16)
    return dot(jnp.concatenate([high, low], axis=1), ones)


def unit_pair(x_ref, offset):
    values = x_ref[:, offset : offset + 2 * HEAD].astype(F32)
    inverse = lax.rsqrt(pair_sum(values * values) + 1e-06)
    return values * inverse, inverse


def unit_back(grad, unit, inverse):
    return inverse * (grad - unit * pair_sum(grad * unit))


def spread(pair):
    swapped = swap(pair)
    left = is_left(ROWS)
    return jnp.where(left, pair, swapped), jnp.where(left, swapped, pair)


def put_spread(ref, pair):
    zero, one = spread(pair)
    ref[:ROWS] = zero.astype(BF16)
    ref[ROWS:] = one.astype(BF16)


def pack_head(array, column):
    cols = slice(column, column + HEAD)
    return [array[:HALF, cols], array[HALF:, cols]]


def unpack_heads(ref, lane):
    return jnp.concatenate([ref[h, :, lane : lane + HEAD] for h in range(HEADS)], axis=1)


def project_kernel(low_ref, up_ref, gain_ref, w_ref, normed_ref, packed_ref):
    hidden = jnp.concatenate([low_ref[:HALF], up_ref[:HALF]], axis=0).astype(F32)
    unit, _ = norm_stats(hidden)
    normed = (unit * gain_ref[0:1, :]).astype(BF16)
    normed_ref[0] = normed[:HALF]
    normed_ref[1] = normed[HALF:]
    projected = dot(normed, w_ref[...]).astype(BF16)
    for h in range(HEADS):
        pieces = []
        for part in range(3):
            pieces += pack_head(projected, part * D + h * HEAD)
        packed_ref[h] = jnp.concatenate(pieces, axis=1)


def value_rows(x_ref):
    values = x_ref[:, 4 * HEAD :].astype(F32)
    swapped = swap(values)
    left = is_left(ROWS)
    return [
        [jnp.where(left, values, 1.0), jnp.where(left, swapped, 1.0)],
        [jnp.where(left, 1.0, swapped), jnp.where(left, 1.0, values)],
    ]


def attend_kernel(scal_ref, x_ref, att_ref, inv_ref, q_s, k_s, v_s):
    factor = scal_ref[0]
    other = scal_ref[2]
    put_spread(q_s, unit_pair(x_ref, 0)[0])
    put_spread(k_s, unit_pair(x_ref, 2 * HEAD)[0])
    values = value_rows(x_ref)
    for a in range(2):
        for b in range(2):
            block = values[a][b] if a == b else values[a][b] * other
            v_s[a, b * ROWS : (b + 1) * ROWS] = block.astype(BF16)
    left = is_left(QT)
    for t in range(ROWS // QT):
        totals = []
        for a in range(2):
            start = a * ROWS + t * QT
            scores = dot_nt(q_s[start : start + QT], k_s[...])
            totals.append(dot(jnp.exp2(scores * factor).astype(BF16), v_s[a]))
        inverse = 1.0 / swap(jnp.where(left, totals[1], totals[0]))
        rows = slice(t * QT, (t + 1) * QT)
        inv_ref[rows] = inverse
        att_ref[rows] = (jnp.where(left, totals[0], totals[1]) * inverse).astype(BF16)


def attend_back_kernel(
    scal_ref, x_ref, grad_ref, att_ref, inv_ref, out_ref, q_s, k_s, v_s, g_s, gd_s
):
    factor = scal_ref[0]
    scale = scal_ref[1]
    other = scal_ref[2]
    left = is_left(ROWS)
    query_unit, query_inverse = unit_pair(x_ref, 0)
    key_unit, key_inverse = unit_pair(x_ref, 2 * HEAD)
    put_spread(q_s, query_unit)
    key_wide = spread(key_unit)
    k_s[:ROWS] = key_wide[0].astype(BF16)
    k_s[ROWS:] = key_wide[1].astype(BF16)
    values = value_rows(x_ref)
    for a in range(2):
        for b in range(2):
            v_s[a, b * ROWS : (b + 1) * ROWS] = values[a][b].astype(BF16)
    grad = grad_ref[...].astype(F32)
    inverse = inv_ref[...]
    delta = swap(pair_sum(grad * att_ref[...].astype(F32)) * inverse)
    high = delta.astype(BF16).astype(F32)
    grad = grad * inverse
    lanes = lax.broadcasted_iota(jnp.int32, (ROWS, 2 * HEAD), 1) & (HEAD - 1)
    tail = jnp.where(lanes == 0, -high, jnp.where(lanes == 1, high - delta, 0.0))
    grad_rows = [jnp.where(left, grad, tail), jnp.where(left, tail, grad)]
    grad_wide = spread(grad)
    for a in range(2):
        rows = slice(a * ROWS, (a + 1) * ROWS)
        for b in range(2):
            mask = 1.0 if a == b else other
            g_s[b, rows] = (grad_rows[a] * mask).astype(BF16)
            gd_s[b, rows] = (grad_wide[a] * mask).astype(BF16)
    dq = [None, None]
    dk = [None, None]
    dv = [None, None]

    def add(sums, place, term):
        sums[place] = term if sums[place] is None else sums[place] + term

    for b in range(2):
        keys = slice(b * ROWS, (b + 1) * ROWS)
        key = k_s[keys]
        key_flat = key_wide[b].T.astype(BF16)
        for a in range(2):
            rows = slice(a * ROWS, (a + 1) * ROWS)
            query = q_s[rows]
            weights = jnp.exp2(dot_nt(key, query) * factor)
            grad_weights = dot_nt(v_s[a, keys], g_s[b, rows])
            grad_scores = (weights * grad_weights).astype(BF16)
            add(dv, b, dot(weights.astype(BF16), gd_s[b, rows]))
            add(dk, b, dot(grad_scores, query))
            add(dq, a, dot(key_flat, grad_scores))
    dq_pair = jnp.where(left, dq[0].T, dq[1].T) * scale
    dk_pair = jnp.where(left, dk[0], dk[1]) * scale
    out_ref[:, : 2 * HEAD] = unit_back(dq_pair, query_unit, query_inverse).astype(BF16)
    out_ref[:, 2 * HEAD : 4 * HEAD] = unit_back(dk_pair, key_unit, key_inverse).astype(BF16)
    out_ref[:, 4 * HEAD :] = jnp.where(left, dv[0], dv[1]).astype(BF16)


def weight_kernel(core_ref, packed_ref, normed_ref, mine_ref, other_ref):
    product = None
    for a in range(2):
        pieces = []
        for part in range(3):
            start = part * 2 * HEAD + a * HEAD
            pieces.append(packed_ref[:, start : start + HEAD])
        normed = jnp.concatenate([normed_ref[i, a] for i in range(8)], axis=0)
        term = dot_tn(normed, jnp.concatenate(pieces, axis=1))
        product = term if product is None else product + term
    first = core_ref[0] == 0
    for g in range(8):
        zero = product[g * 64 : g * 64 + 32]
        one = product[g * 64 + 32 : g * 64 + 64]
        mine_ref[g] = jnp.where(first, zero, one).astype(BF16)
        other_ref[g] = jnp.where(first, one, zero).astype(BF16)


def pair_kernel(x_ref, mine_ref, theirs_ref, zero_ref, one_ref, two_ref, three_ref):
    for k, ref in enumerate((zero_ref, one_ref, two_ref, three_ref)):
        block = pl.ds(((x_ref[0] + k) & 3) * 2, 2)
        ref[...] = (mine_ref[block].astype(F32) + theirs_ref[block].astype(F32)).astype(BF16)


def join_kernel(part_ref, zero_ref, one_ref, two_ref, three_ref, out_ref):
    for z in range(2):
        narrow = part_ref[z, :, : 5 * D].astype(F32)
        qkv = zero_ref[z].astype(F32)
        for ref in (one_ref, two_ref, three_ref):
            qkv = qkv + ref[z].astype(F32)
        for j in range(8):
            rows = slice(4 * j, 4 * j + 4)
            out_ref[z * 8 + j, :, : 5 * D] = narrow[rows].astype(BF16)
            start = 5 * D + D * (j // 2)
            down = part_ref[z, 16 * (j % 2) : 16 * (j % 2) + 16, start : start + D].astype(F32)
            for s in range(4):
                cols = slice((5 + s) * D, (6 + s) * D)
                out_ref[z * 8 + j, :, cols] = down[4 * s : 4 * s + 4].astype(BF16)
            padded = jnp.concatenate([qkv[rows], jnp.zeros((4, HEAD), F32)], axis=1)
            out_ref[z * 8 + j, :, 9 * D :] = padded.astype(BF16)


def last_kernel(
    got_ref, qkv_rows_ref, up_rows_ref, gains_ref, qkv_ref, out_ref, up_ref, down_ref, gain_ref
):
    grad_scale = 1.0 / math.sqrt(OWN * 128)
    total = got_ref[0, :, : 9 * D].astype(F32)
    for i in range(1, 16):
        total = total + got_ref[i, :, : 9 * D].astype(F32)
    total = total * grad_scale
    out_ref[...] = total[:, :D]
    up = total[:, D : 5 * D]
    up_ref[...] = up
    for s in range(4):
        down_ref[4 * s : 4 * s + 4] = total[:, (5 + s) * D : (6 + s) * D]
    heads = []
    for h in range(HEADS):
        pair = got_ref[h, :, 9 * D :].astype(F32) + got_ref[8 + h, :, 9 * D :].astype(F32)
        heads.append(pair * grad_scale)
    pieces = [heads[h][:, p * HEAD : (p + 1) * HEAD] for p in range(3) for h in range(HEADS)]
    qkv = jnp.concatenate(pieces, axis=1)
    qkv_ref[...] = qkv
    eye = lax.broadcasted_iota(jnp.int32, (4, 4), 0) == lax.broadcasted_iota(
        jnp.int32, (4, 4), 1
    )
    products = (qkv * qkv_rows_ref[...].astype(F32), up * up_rows_ref[...].astype(F32))
    for i, product in enumerate(products):
        column = jnp.sum(product, axis=1, keepdims=True)
        row = jnp.sum(jnp.where(eye, column, 0.0), axis=0, keepdims=True)
        gain_ref[i : i + 1] = row / gains_ref[i : i + 1]


def load_all(pairs, sems):
    loads = [
        pltpu.make_async_copy(source, target, sems.at[i])
        for i, (source, target) in enumerate(pairs)
    ]
    for load in loads:
        load.start()
    return loads


def near_kernel(*refs):
    count = (len(refs) - 1) // 2
    for load in load_all(tuple(zip(refs[:count], refs[count:-1])), refs[-1]):
        load.wait()


def enter_kernel(
    field_hbm, mask_hbm, embed_hbm, cot_hbm, low_ref, up_ref,
    field_ref, mask_ref, embed_ref, cot_ref, sems,
):
    loads = load_all(
        (
            (mask_hbm, mask_ref),
            (embed_hbm, embed_ref),
            (field_hbm, field_ref),
            (cot_hbm, cot_ref),
        ),
        sems,
    )
    for load in loads:
        load.wait()
    sea = embed_ref[0:1].astype(F32)
    land = embed_ref[1:2].astype(F32)
    mask = (mask_ref[...] == 1).astype(F32)
    eye = lax.broadcasted_iota(jnp.int32, (16, 16), 0) == lax.broadcasted_iota(
        jnp.int32, (16, 16), 1
    )
    for row in range(4):
        column = jnp.sum(jnp.where(eye, mask[row : row + 1], 0.0), axis=1, keepdims=True)
        chosen = jnp.where(column > 0.5, land, sea)
        ref = up_ref if row < 2 else low_ref
        for level in range(3):
            start = (level * 2 + row % 2) * 16
            rows = slice(start, start + 16)
            ref[rows] = (field_ref[level, row].astype(F32) + chosen).astype(BF16)
            ref[HALF + start : HALF + start + 16] = cot_ref[level, row]


def core_columns(array, width, core):
    pieces = [
        array[:, (2 * g + core) * width : (2 * g + core + 1) * width] for g in range(8)
    ]
    return jnp.concatenate(pieces, axis=1)


def middle_kernel(
    core_ref, att_ref, low_ref, up_ref, gain_ref, w_out_ref, w_up_ref, w_down_ref,
    out_low_ref, out_up_ref, packed_ref, gm_ref, send_ref, keep_ref,
):
    first = core_ref[0] == 0
    attended = jnp.concatenate([unpack_heads(att_ref, 0), unpack_heads(att_ref, HEAD)], axis=0)
    hidden = jnp.concatenate([low_ref[:HALF], up_ref[:HALF]], axis=0).astype(F32)
    cot = jnp.concatenate([low_ref[HALF:], up_ref[HALF:]], axis=0)
    gain = gain_ref[1:2, :]
    mixed = (hidden + dot(attended, w_out_ref[...])).astype(BF16).astype(F32)
    unit, inverse = norm_stats(mixed)
    normed = (unit * gain).astype(BF16)
    pre = dot(normed, w_up_ref[...])
    root = math.sqrt(2.0 / math.pi)
    square = pre * pre
    bend = jnp.tanh(root * pre * (1.0 + 0.044715 * square))
    half_up = 0.5 * (1.0 + bend)
    activated = (pre * half_up).astype(BF16)
    slope = half_up + 0.5 * pre * (1.0 - bend * bend) * root * (1.0 + 3 * 0.044715 * square)
    grad_pre = (dot_nt(cot, w_down_ref[...]) * slope).astype(BF16)
    grad_normed = dot_nt(grad_pre, w_up_ref[...])
    grad_mixed = cot.astype(F32) + norm_back(grad_normed, unit, inverse, gain)
    gm_ref[...] = grad_mixed
    grad_low = grad_mixed.astype(BF16)
    grad_attended = dot_nt(grad_low, w_out_ref[...]).astype(BF16)
    for h in range(HEADS):
        packed_ref[h] = jnp.concatenate(pack_head(grad_attended, h * HEAD), axis=1)
    layer_out = (mixed + dot(activated, w_down_ref[...])).astype(BF16)
    out_low_ref[...] = layer_out[:HALF]
    out_up_ref[...] = layer_out[HALF:]
    start = 0
    for array, width in ((activated, 128), (normed, 32), (attended, 32)):
        zero = core_columns(array, width, 0)
        one = core_columns(array, width, 1)
        cols = slice(start, start + 8 * width)
        keep_ref[:, cols] = jnp.where(first, zero, one)
        send_ref[:, cols] = jnp.where(first, one, zero)
        start += 8 * width
    for array in (cot, grad_pre, grad_low):
        send_ref[:, start : start + array.shape[1]] = array
        start += array.shape[1]


def partial_kernel(keep_ref, sent_ref, got_ref, out_ref):
    def both(own_ref, start, width):
        cols = slice(start, start + width)
        return jnp.concatenate([own_ref[:, cols], got_ref[:, cols]], axis=0)

    product = dot_tn(both(keep_ref, 0, 2 * D), both(sent_ref, 3 * D, D)).astype(BF16)
    for g in range(8):
        for s in range(4):
            at = g * 128 + s * 32
            out_ref[g, :, (5 + s) * D : (6 + s) * D] = product[at : at + 32]
    product = dot_tn(both(keep_ref, 2 * D, D // 2), both(sent_ref, 4 * D, FF)).astype(BF16)
    for g in range(8):
        out_ref[g, :, D : 5 * D] = product[g * 32 : g * 32 + 32]
    product = dot_tn(both(keep_ref, 5 * D // 2, D // 2), both(sent_ref, 8 * D, D)).astype(BF16)
    for g in range(8):
        out_ref[g, :, :D] = product[g * 32 : g * 32 + 32]


def input_grad_kernel(
    packed_ref, low_ref, up_ref, gain_ref, gm_ref, w_ref, glow_ref, gup_ref
):
    halves = []
    for a in range(2):
        parts = [unpack_heads(packed_ref, place * 128 + a * HEAD) for place in range(3)]
        halves.append(jnp.concatenate(parts, axis=1))
    grad_projected = jnp.concatenate(halves, axis=0)
    hidden = jnp.concatenate([low_ref[:HALF], up_ref[:HALF]], axis=0).astype(F32)
    unit, inverse = norm_stats(hidden)
    grad_normed = dot_nt(grad_projected, w_ref[...])
    grad = gm_ref[...] + norm_back(grad_normed, unit, inverse, gain_ref[0:1, :])
    grad = grad.astype(BF16)
    glow_ref[...] = grad[:HALF]
    gup_ref[...] = grad[HALF:]


VMEM = pl.BlockSpec(memory_space=pltpu.VMEM)
SMEM = pl.BlockSpec(memory_space=pltpu.SMEM)
ANY = pl.BlockSpec(memory_space=pl.ANY)


def call(kernel, outs, specs, scratch=(), vmem=12, cost=3_000_000):
    shapes = tuple(jax.ShapeDtypeStruct(shape, dtype) for shape, dtype in outs)
    return pl.pallas_call(
        kernel,
        out_shape=shapes,
        in_specs=specs,
        out_specs=(VMEM,) * len(outs),
        scratch_shapes=list(scratch),
        compiler_params=pltpu.CompilerParams(vmem_limit_bytes=vmem * 1024 * 1024),
        cost_estimate=pl.CostEstimate(flops=0, bytes_accessed=cost, transcendentals=0),
    )


def shards(
    fields, land_sea, surface_embed, norm_gains, w_qkv, head_scales, w_out, w_up, w_down, cotangent
):
    lat = lax.axis_index(LAT)
    lon = lax.axis_index(LON)
    device = lax.axis_index(ALL)
    core = lax.axis_index("c").astype(jnp.int32).reshape(1)
    x_index = lax.axis_index("x").astype(jnp.int32).reshape(1)
    forward = [(i, (i + 1) % 16) for i in range(16)]
    backward = [(j, i) for i, j in forward]
    across = [(0, 1), (1, 0)]
    half = ((HALF, D), BF16)
    low, up = call(
        enter_kernel,
        [((OWN, D), BF16)] * 2,
        [ANY] * 4,
        [
            pltpu.VMEM((3, 4, 16, D), BF16),
            pltpu.VMEM((4, 16), jnp.int32),
            pltpu.VMEM((2, D), BF16),
            pltpu.VMEM((3, 4, 16, D), BF16),
            pltpu.SemaphoreType.DMA((4,)),
        ],
        vmem=60,
    )(fields, land_sea, surface_embed, cotangent)
    low = lax.ppermute(low, LAT, forward)
    w_qkv_near, gains_near = call(
        near_kernel,
        [((D, 3 * D), BF16), ((2, D), F32)],
        [ANY] * 2,
        [pltpu.SemaphoreType.DMA((2,))],
    )(w_qkv, norm_gains)
    low, w_qkv_near, gains_near = lax.optimization_barrier((low, w_qkv_near, gains_near))

    scale = head_scales[lon]
    valid = jnp.where(lat == 0, 0.0, 1.0)
    scal = jnp.stack([scale * (0.5 * math.log2(math.e)), scale, valid]).astype(F32)
    rows_qkv = lax.dynamic_slice_in_dim(w_qkv, device * 4, 4, axis=0)
    rows_up = lax.dynamic_slice_in_dim(w_up, device * 4, 4, axis=0)
    gains = lax.dynamic_slice_in_dim(norm_gains, device * 4, 4, axis=1)

    normed, packed = call(
        project_kernel,
        [((2, HALF, D), BF16), ((HEADS, HALF, 384), BF16)],
        [VMEM] * 4,
        vmem=12,
        cost=8_000_000,
    )(low, up, gains_near, w_qkv_near)
    heads = lax.all_to_all(packed, LON, 0, 0, tiled=True).reshape(ROWS, 384)
    heads, scal, rows_qkv, rows_up, gains = lax.optimization_barrier(
        (heads, scal, rows_qkv, rows_up, gains)
    )
    heads, normed = lax.optimization_barrier((heads, normed))
    normed_all = lax.all_gather(normed, LON, axis=0, tiled=False)

    wide = 2 * ROWS
    att, inv = call(
        attend_kernel,
        [((ROWS, 128), BF16), ((ROWS, 128), F32)],
        [SMEM, VMEM],
        [
            pltpu.VMEM((wide, 128), BF16),
            pltpu.VMEM((wide, 128), BF16),
            pltpu.VMEM((2, wide, 128), BF16),
        ],
        vmem=20,
        cost=20_000_000,
    )(scal, heads)
    att_rows = lax.all_to_all(att.reshape(HEADS, HALF, 128), LON, 0, 0, tiled=True)

    out_low, out_up, packed_grad, grad_mixed, sent, keep = call(
        middle_kernel,
        [
            half,
            half,
            ((HEADS, HALF, 128), BF16),
            ((OWN, D), F32),
            ((OWN, 9 * D), BF16),
            ((OWN, 3 * D), BF16),
        ],
        [SMEM] + [VMEM] * 7,
        vmem=24,
    )(core, att_rows, low, up, gains_near, w_out, w_up, w_down)
    grad_heads = lax.all_to_all(packed_grad, LON, 0, 0, tiled=True).reshape(ROWS, 128)
    received = lax.ppermute(sent, "c", across)
    out_back = lax.ppermute(out_low, LAT, backward)
    (pair,) = call(partial_kernel, [((8, 32, 9 * D), BF16)], [VMEM] * 3, vmem=24)(
        keep, sent, received
    )
    part = lax.psum_scatter(pair, "x", scatter_dimension=0, tiled=True)

    block = ((8, 32, 192), BF16)
    (packed_back,) = call(
        attend_back_kernel,
        [((ROWS, 384), BF16)],
        [SMEM] + [VMEM] * 4,
        [
            pltpu.VMEM((wide, 128), BF16),
            pltpu.VMEM((wide, 128), BF16),
            pltpu.VMEM((2, wide, 128), BF16),
            pltpu.VMEM((2, wide, 128), BF16),
            pltpu.VMEM((2, wide, 128), BF16),
        ],
        vmem=32,
        cost=1_000_000_000,
    )(scal, heads, grad_heads, att, inv)
    packed_back, out_back = lax.optimization_barrier((packed_back, out_back))
    grad_packed = lax.all_to_all(
        packed_back.reshape(HEADS, HALF, 384), LON, 0, 0, tiled=True
    )
    mine, other = call(weight_kernel, [block] * 2, [SMEM] + [VMEM] * 2)(
        core, packed_back, normed_all
    )
    theirs = lax.ppermute(other, "c", across)
    blocks = call(pair_kernel, [((2, 32, 192), BF16)] * 4, [SMEM, VMEM, VMEM])(
        x_index, mine, theirs
    )
    blocks = [blocks[0]] + [
        lax.ppermute(blocks[k], "x", [(i, (i + k) % 4) for i in range(4)]) for k in (1, 2, 3)
    ]
    grad_low, grad_up = call(
        input_grad_kernel,
        [half] * 2,
        [VMEM] * 6,
        vmem=12,
    )(grad_packed, low, up, gains_near, grad_mixed, w_qkv_near)

    part, grad_low, grad_up = lax.optimization_barrier((part, grad_low, grad_up))
    grad_back = lax.ppermute(grad_low, LAT, backward)
    (joined,) = call(join_kernel, [((16, 4, 9 * D + 256), BF16)], [VMEM] * 5)(part, *blocks)
    got = lax.all_to_all(joined, ("zh",) + LON, 0, 0, tiled=True)
    grad_qkv, grad_out, grad_up_w, grad_down, grad_gains = call(
        last_kernel,
        [
            ((4, 3 * D), F32),
            ((4, D), F32),
            ((4, FF), F32),
            ((16, D), F32),
            ((2, 4), F32),
        ],
        [VMEM] * 4,
    )(got, rows_qkv, rows_up, gains)

    def place(own, moved):
        shape = (3, 2, 16, D)
        return jnp.concatenate([own.reshape(shape), moved.reshape(shape)], axis=1)

    return (
        place(out_up, out_back),
        place(grad_up, grad_back),
        grad_qkv,
        grad_out,
        grad_up_w,
        grad_down,
        grad_gains,
    )


def solution(mesh):
    fine = Mesh(mesh.devices.reshape(AXIS_SIZES), ALL)
    grid = P(None, LAT, LON, None)
    in_specs = (grid, P(LAT, LON), P(), P(), P(), P(), P(), P(), P(), grid)
    rows = P(ALL, None)
    out_specs = (grid, grid, rows, rows, rows, rows, P(None, ALL))
    return jax.shard_map(shards, mesh=fine, in_specs=in_specs, out_specs=out_specs, check_vma=False)
```

```python
import math

import jax
import jax.numpy as jnp
from jax import lax
from jax.experimental import pallas as pl
from jax.experimental.pallas import tpu as pltpu
from jax.sharding import Mesh
from jax.sharding import PartitionSpec as P

LAT = ("x", "zh", "c")
LON = ("zl", "y")
ALL = LAT + LON
AXIS_SIZES = (4, 2, 2, 2, 4)

HEADS = 8
HEAD = 64
D = 512
FF = 2048
HALF = 96
ROWS = 768
OWN = 2 * HALF
QT = 256

F32 = jnp.float32
BF16 = jnp.bfloat16
NT = (((1,), (1,)), ((), ()))
TN = (((0,), (0,)), ((), ()))


def dot(a, b):
    return jnp.dot(a, b, preferred_element_type=F32)


def dot_nt(a, b):
    return lax.dot_general(a, b, NT, preferred_element_type=F32)


def dot_tn(a, b):
    return lax.dot_general(a, b, TN, preferred_element_type=F32)


def norm_stats(values):
    centred = values - jnp.mean(values, axis=-1, keepdims=True)
    variance = jnp.mean(centred * centred, axis=-1, keepdims=True)
    inverse = lax.rsqrt(variance + 1e-05)
    return centred * inverse, inverse


def norm_back(grad, unit, inverse, gain):
    scaled = grad * gain
    first = jnp.mean(scaled, axis=-1, keepdims=True)
    second = jnp.mean(scaled * unit, axis=-1, keepdims=True)
    return inverse * (scaled - first - unit * second)


def swap(pair):
    return pltpu.roll(pair, HEAD, axis=1)


def is_left(rows):
    return lax.broadcasted_iota(jnp.int32, (rows, 2 * HEAD), 1) < HEAD


def pair_sum(values):
    row = lax.broadcasted_iota(jnp.int32, (4 * HEAD, 2 * HEAD), 0) >> 6
    column = lax.broadcasted_iota(jnp.int32, (4 * HEAD, 2 * HEAD), 1) >> 6
    ones = jnp.where((row & 1) == column, 1.0, 0.0).astype(BF16)
    high = values.astype(BF16)
    low = (values - high.astype(F32)).astype(BF16)
    return dot(jnp.concatenate([high, low], axis=1), ones)


def unit_pair(x_ref, offset):
    values = x_ref[:, offset : offset + 2 * HEAD].astype(F32)
    inverse = lax.rsqrt(pair_sum(values * values) + 1e-06)
    return values * inverse, inverse


def unit_back(grad, unit, inverse):
    return inverse * (grad - unit * pair_sum(grad * unit))


def spread(pair):
    swapped = swap(pair)
    left = is_left(ROWS)
    return jnp.where(left, pair, swapped), jnp.where(left, swapped, pair)


def put_spread(ref, pair):
    zero, one = spread(pair)
    ref[:ROWS] = zero.astype(BF16)
    ref[ROWS:] = one.astype(BF16)


def pack_head(array, column):
    cols = slice(column, column + HEAD)
    return [array[:HALF, cols], array[HALF:, cols]]


def unpack_heads(ref, lane):
    return jnp.concatenate([ref[h, :, lane : lane + HEAD] for h in range(HEADS)], axis=1)


def project_kernel(low_ref, up_ref, gain_ref, w_ref, normed_ref, packed_ref):
    hidden = jnp.concatenate([low_ref[:HALF], up_ref[:HALF]], axis=0).astype(F32)
    unit, _ = norm_stats(hidden)
    normed = (unit * gain_ref[0:1, :]).astype(BF16)
    normed_ref[0] = normed[:HALF]
    normed_ref[1] = normed[HALF:]
    projected = dot(normed, w_ref[...]).astype(BF16)
    for h in range(HEADS):
        pieces = []
        for part in range(3):
            pieces += pack_head(projected, part * D + h * HEAD)
        packed_ref[h] = jnp.concatenate(pieces, axis=1)


def value_rows(x_ref):
    values = x_ref[:, 4 * HEAD :].astype(F32)
    swapped = swap(values)
    left = is_left(ROWS)
    return [
        [jnp.where(left, values, 1.0), jnp.where(left, swapped, 1.0)],
        [jnp.where(left, 1.0, swapped), jnp.where(left, 1.0, values)],
    ]


def attend_kernel(scal_ref, x_ref, att_ref, inv_ref, q_s, k_s, v_s):
    factor = scal_ref[0]
    other = scal_ref[2]
    put_spread(q_s, unit_pair(x_ref, 0)[0])
    put_spread(k_s, unit_pair(x_ref, 2 * HEAD)[0])
    values = value_rows(x_ref)
    for a in range(2):
        for b in range(2):
            block = values[a][b] if a == b else values[a][b] * other
            v_s[a, b * ROWS : (b + 1) * ROWS] = block.astype(BF16)
    left = is_left(QT)
    for t in range(ROWS // QT):
        totals = []
        for a in range(2):
            start = a * ROWS + t * QT
            scores = dot_nt(q_s[start : start + QT], k_s[...])
            totals.append(dot(jnp.exp2(scores * factor).astype(BF16), v_s[a]))
        inverse = 1.0 / swap(jnp.where(left, totals[1], totals[0]))
        rows = slice(t * QT, (t + 1) * QT)
        inv_ref[rows] = inverse
        att_ref[rows] = (jnp.where(left, totals[0], totals[1]) * inverse).astype(BF16)


def attend_back_kernel(
    scal_ref, x_ref, grad_ref, att_ref, inv_ref, out_ref, q_s, k_s, v_s, g_s, gd_s
):
    factor = scal_ref[0]
    scale = scal_ref[1]
    other = scal_ref[2]
    left = is_left(ROWS)
    query_unit, query_inverse = unit_pair(x_ref, 0)
    key_unit, key_inverse = unit_pair(x_ref, 2 * HEAD)
    put_spread(q_s, query_unit)
    key_wide = spread(key_unit)
    k_s[:ROWS] = key_wide[0].astype(BF16)
    k_s[ROWS:] = key_wide[1].astype(BF16)
    values = value_rows(x_ref)
    for a in range(2):
        for b in range(2):
            v_s[a, b * ROWS : (b + 1) * ROWS] = values[a][b].astype(BF16)
    grad = grad_ref[...].astype(F32)
    inverse = inv_ref[...]
    delta = swap(pair_sum(grad * att_ref[...].astype(F32)) * inverse)
    high = delta.astype(BF16).astype(F32)
    grad = grad * inverse
    lanes = lax.broadcasted_iota(jnp.int32, (ROWS, 2 * HEAD), 1) & (HEAD - 1)
    tail = jnp.where(lanes == 0, -high, jnp.where(lanes == 1, high - delta, 0.0))
    grad_rows = [jnp.where(left, grad, tail), jnp.where(left, tail, grad)]
    grad_wide = spread(grad)
    for a in range(2):
        rows = slice(a * ROWS, (a + 1) * ROWS)
        for b in range(2):
            mask = 1.0 if a == b else other
            g_s[b, rows] = (grad_rows[a] * mask).astype(BF16)
            gd_s[b, rows] = (grad_wide[a] * mask).astype(BF16)
    dq = [None, None]
    dk = [None, None]
    dv = [None, None]

    def add(sums, place, term):
        sums[place] = term if sums[place] is None else sums[place] + term

    for b in range(2):
        keys = slice(b * ROWS, (b + 1) * ROWS)
        key = k_s[keys]
        key_flat = key_wide[b].T.astype(BF16)
        for a in range(2):
            rows = slice(a * ROWS, (a + 1) * ROWS)
            query = q_s[rows]
            weights = jnp.exp2(dot_nt(key, query) * factor)
            grad_weights = dot_nt(v_s[a, keys], g_s[b, rows])
            grad_scores = (weights * grad_weights).astype(BF16)
            add(dv, b, dot(weights.astype(BF16), gd_s[b, rows]))
            add(dk, b, dot(grad_scores, query))
            add(dq, a, dot(key_flat, grad_scores))
    dq_pair = jnp.where(left, dq[0].T, dq[1].T) * scale
    dk_pair = jnp.where(left, dk[0], dk[1]) * scale
    out_ref[:, : 2 * HEAD] = unit_back(dq_pair, query_unit, query_inverse).astype(BF16)
    out_ref[:, 2 * HEAD : 4 * HEAD] = unit_back(dk_pair, key_unit, key_inverse).astype(BF16)
    out_ref[:, 4 * HEAD :] = jnp.where(left, dv[0], dv[1]).astype(BF16)


def weight_kernel(core_ref, packed_ref, normed_ref, mine_ref, other_ref):
    product = None
    for a in range(2):
        pieces = []
        for part in range(3):
            start = part * 2 * HEAD + a * HEAD
            pieces.append(packed_ref[:, start : start + HEAD])
        normed = jnp.concatenate([normed_ref[i, a] for i in range(8)], axis=0)
        term = dot_tn(normed, jnp.concatenate(pieces, axis=1))
        product = term if product is None else product + term
    first = core_ref[0] == 0
    for g in range(8):
        zero = product[g * 64 : g * 64 + 32]
        one = product[g * 64 + 32 : g * 64 + 64]
        mine_ref[g] = jnp.where(first, zero, one).astype(BF16)
        other_ref[g] = jnp.where(first, one, zero).astype(BF16)


def pair_kernel(x_ref, mine_ref, theirs_ref, zero_ref, one_ref, two_ref, three_ref):
    for k, ref in enumerate((zero_ref, one_ref, two_ref, three_ref)):
        block = pl.ds(((x_ref[0] + k) & 3) * 2, 2)
        ref[...] = (mine_ref[block].astype(F32) + theirs_ref[block].astype(F32)).astype(BF16)


def join_kernel(part_ref, zero_ref, one_ref, two_ref, three_ref, out_ref):
    for z in range(2):
        narrow = part_ref[z, :, : 5 * D].astype(F32)
        qkv = zero_ref[z].astype(F32)
        for ref in (one_ref, two_ref, three_ref):
            qkv = qkv + ref[z].astype(F32)
        for j in range(8):
            rows = slice(4 * j, 4 * j + 4)
            out_ref[z * 8 + j, :, : 5 * D] = narrow[rows].astype(BF16)
            start = 5 * D + D * (j // 2)
            down = part_ref[z, 16 * (j % 2) : 16 * (j % 2) + 16, start : start + D].astype(F32)
            for s in range(4):
                cols = slice((5 + s) * D, (6 + s) * D)
                out_ref[z * 8 + j, :, cols] = down[4 * s : 4 * s + 4].astype(BF16)
            padded = jnp.concatenate([qkv[rows], jnp.zeros((4, HEAD), F32)], axis=1)
            out_ref[z * 8 + j, :, 9 * D :] = padded.astype(BF16)


def last_kernel(
    got_ref, qkv_rows_ref, up_rows_ref, gains_ref, qkv_ref, out_ref, up_ref, down_ref, gain_ref
):
    grad_scale = 1.0 / math.sqrt(OWN * 128)
    total = got_ref[0, :, : 9 * D].astype(F32)
    for i in range(1, 16):
        total = total + got_ref[i, :, : 9 * D].astype(F32)
    total = total * grad_scale
    out_ref[...] = total[:, :D]
    up = total[:, D : 5 * D]
    up_ref[...] = up
    for s in range(4):
        down_ref[4 * s : 4 * s + 4] = total[:, (5 + s) * D : (6 + s) * D]
    heads = []
    for h in range(HEADS):
        pair = got_ref[h, :, 9 * D :].astype(F32) + got_ref[8 + h, :, 9 * D :].astype(F32)
        heads.append(pair * grad_scale)
    pieces = [heads[h][:, p * HEAD : (p + 1) * HEAD] for p in range(3) for h in range(HEADS)]
    qkv = jnp.concatenate(pieces, axis=1)
    qkv_ref[...] = qkv
    eye = lax.broadcasted_iota(jnp.int32, (4, 4), 0) == lax.broadcasted_iota(
        jnp.int32, (4, 4), 1
    )
    products = (qkv * qkv_rows_ref[...].astype(F32), up * up_rows_ref[...].astype(F32))
    for i, product in enumerate(products):
        column = jnp.sum(product, axis=1, keepdims=True)
        row = jnp.sum(jnp.where(eye, column, 0.0), axis=0, keepdims=True)
        gain_ref[i : i + 1] = row / gains_ref[i : i + 1]


def load_all(pairs, sems):
    loads = [
        pltpu.make_async_copy(source, target, sems.at[i])
        for i, (source, target) in enumerate(pairs)
    ]
    for load in loads:
        load.start()
    return loads


def near_kernel(*refs):
    count = (len(refs) - 1) // 2
    for load in load_all(tuple(zip(refs[:count], refs[count:-1])), refs[-1]):
        load.wait()


def enter_kernel(
    field_hbm, mask_hbm, embed_hbm, cot_hbm, low_ref, up_ref,
    field_ref, mask_ref, embed_ref, cot_ref, sems,
):
    loads = load_all(
        (
            (mask_hbm, mask_ref),
            (embed_hbm, embed_ref),
            (field_hbm, field_ref),
            (cot_hbm, cot_ref),
        ),
        sems,
    )
    for load in loads:
        load.wait()
    sea = embed_ref[0:1].astype(F32)
    land = embed_ref[1:2].astype(F32)
    mask = (mask_ref[...] == 1).astype(F32)
    eye = lax.broadcasted_iota(jnp.int32, (16, 16), 0) == lax.broadcasted_iota(
        jnp.int32, (16, 16), 1
    )
    for row in range(4):
        column = jnp.sum(jnp.where(eye, mask[row : row + 1], 0.0), axis=1, keepdims=True)
        chosen = jnp.where(column > 0.5, land, sea)
        ref = up_ref if row < 2 else low_ref
        for level in range(3):
            start = (level * 2 + row % 2) * 16
            rows = slice(start, start + 16)
            ref[rows] = (field_ref[level, row].astype(F32) + chosen).astype(BF16)
            ref[HALF + start : HALF + start + 16] = cot_ref[level, row]


def core_columns(array, width, core):
    pieces = [
        array[:, (2 * g + core) * width : (2 * g + core + 1) * width] for g in range(8)
    ]
    return jnp.concatenate(pieces, axis=1)


def middle_kernel(
    core_ref, att_ref, low_ref, up_ref, gain_ref, w_out_ref, w_up_ref, w_down_ref,
    out_low_ref, out_up_ref, packed_ref, gm_ref, send_ref, keep_ref,
):
    first = core_ref[0] == 0
    attended = jnp.concatenate([unpack_heads(att_ref, 0), unpack_heads(att_ref, HEAD)], axis=0)
    hidden = jnp.concatenate([low_ref[:HALF], up_ref[:HALF]], axis=0).astype(F32)
    cot = jnp.concatenate([low_ref[HALF:], up_ref[HALF:]], axis=0)
    gain = gain_ref[1:2, :]
    mixed = (hidden + dot(attended, w_out_ref[...])).astype(BF16).astype(F32)
    unit, inverse = norm_stats(mixed)
    normed = (unit * gain).astype(BF16)
    pre = dot(normed, w_up_ref[...])
    root = math.sqrt(2.0 / math.pi)
    square = pre * pre
    bend = jnp.tanh(root * pre * (1.0 + 0.044715 * square))
    half_up = 0.5 * (1.0 + bend)
    activated = (pre * half_up).astype(BF16)
    slope = half_up + 0.5 * pre * (1.0 - bend * bend) * root * (1.0 + 3 * 0.044715 * square)
    grad_pre = (dot_nt(cot, w_down_ref[...]) * slope).astype(BF16)
    grad_normed = dot_nt(grad_pre, w_up_ref[...])
    grad_mixed = cot.astype(F32) + norm_back(grad_normed, unit, inverse, gain)
    gm_ref[...] = grad_mixed
    grad_low = grad_mixed.astype(BF16)
    grad_attended = dot_nt(grad_low, w_out_ref[...]).astype(BF16)
    for h in range(HEADS):
        packed_ref[h] = jnp.concatenate(pack_head(grad_attended, h * HEAD), axis=1)
    layer_out = (mixed + dot(activated, w_down_ref[...])).astype(BF16)
    out_low_ref[...] = layer_out[:HALF]
    out_up_ref[...] = layer_out[HALF:]
    start = 0
    for array, width in ((activated, 128), (normed, 32), (attended, 32)):
        zero = core_columns(array, width, 0)
        one = core_columns(array, width, 1)
        cols = slice(start, start + 8 * width)
        keep_ref[:, cols] = jnp.where(first, zero, one)
        send_ref[:, cols] = jnp.where(first, one, zero)
        start += 8 * width
    for array in (cot, grad_pre, grad_low):
        send_ref[:, start : start + array.shape[1]] = array
        start += array.shape[1]


def partial_kernel(keep_ref, sent_ref, got_ref, out_ref):
    def both(own_ref, start, width):
        cols = slice(start, start + width)
        return jnp.concatenate([own_ref[:, cols], got_ref[:, cols]], axis=0)

    product = dot_tn(both(keep_ref, 0, 2 * D), both(sent_ref, 3 * D, D)).astype(BF16)
    for g in range(8):
        for s in range(4):
            at = g * 128 + s * 32
            out_ref[g, :, (5 + s) * D : (6 + s) * D] = product[at : at + 32]
    product = dot_tn(both(keep_ref, 2 * D, D // 2), both(sent_ref, 4 * D, FF)).astype(BF16)
    for g in range(8):
        out_ref[g, :, D : 5 * D] = product[g * 32 : g * 32 + 32]
    product = dot_tn(both(keep_ref, 5 * D // 2, D // 2), both(sent_ref, 8 * D, D)).astype(BF16)
    for g in range(8):
        out_ref[g, :, :D] = product[g * 32 : g * 32 + 32]


def input_grad_kernel(
    packed_ref, low_ref, up_ref, gain_ref, gm_ref, w_ref, glow_ref, gup_ref
):
    halves = []
    for a in range(2):
        parts = [unpack_heads(packed_ref, place * 128 + a * HEAD) for place in range(3)]
        halves.append(jnp.concatenate(parts, axis=1))
    grad_projected = jnp.concatenate(halves, axis=0)
    hidden = jnp.concatenate([low_ref[:HALF], up_ref[:HALF]], axis=0).astype(F32)
    unit, inverse = norm_stats(hidden)
    grad_normed = dot_nt(grad_projected, w_ref[...])
    grad = gm_ref[...] + norm_back(grad_normed, unit, inverse, gain_ref[0:1, :])
    grad = grad.astype(BF16)
    glow_ref[...] = grad[:HALF]
    gup_ref[...] = grad[HALF:]


VMEM = pl.BlockSpec(memory_space=pltpu.VMEM)
SMEM = pl.BlockSpec(memory_space=pltpu.SMEM)
ANY = pl.BlockSpec(memory_space=pl.ANY)


def call(kernel, outs, specs, scratch=(), vmem=12, cost=3_000_000):
    shapes = tuple(jax.ShapeDtypeStruct(shape, dtype) for shape, dtype in outs)
    return pl.pallas_call(
        kernel,
        out_shape=shapes,
        in_specs=specs,
        out_specs=(VMEM,) * len(outs),
        scratch_shapes=list(scratch),
        compiler_params=pltpu.CompilerParams(vmem_limit_bytes=vmem * 1024 * 1024),
        cost_estimate=pl.CostEstimate(flops=0, bytes_accessed=cost, transcendentals=0),
    )


def shards(
    fields, land_sea, surface_embed, norm_gains, w_qkv, head_scales, w_out, w_up, w_down, cotangent
):
    lat = lax.axis_index(LAT)
    lon = lax.axis_index(LON)
    device = lax.axis_index(ALL)
    core = lax.axis_index("c").astype(jnp.int32).reshape(1)
    x_index = lax.axis_index("x").astype(jnp.int32).reshape(1)
    forward = [(i, (i + 1) % 16) for i in range(16)]
    backward = [(j, i) for i, j in forward]
    across = [(0, 1), (1, 0)]
    half = ((HALF, D), BF16)
    low, up = call(
        enter_kernel,
        [((OWN, D), BF16)] * 2,
        [ANY] * 4,
        [
            pltpu.VMEM((3, 4, 16, D), BF16),
            pltpu.VMEM((4, 16), jnp.int32),
            pltpu.VMEM((2, D), BF16),
            pltpu.VMEM((3, 4, 16, D), BF16),
            pltpu.SemaphoreType.DMA((4,)),
        ],
        vmem=60,
    )(fields, land_sea, surface_embed, cotangent)
    low = lax.ppermute(low, LAT, forward)
    w_qkv_near, gains_near = call(
        near_kernel,
        [((D, 3 * D), BF16), ((2, D), F32)],
        [ANY] * 2,
        [pltpu.SemaphoreType.DMA((2,))],
    )(w_qkv, norm_gains)
    low, w_qkv_near, gains_near = lax.optimization_barrier((low, w_qkv_near, gains_near))

    scale = head_scales[lon]
    valid = jnp.where(lat == 0, 0.0, 1.0)
    scal = jnp.stack([scale * (0.5 * math.log2(math.e)), scale, valid]).astype(F32)
    rows_qkv = lax.dynamic_slice_in_dim(w_qkv, device * 4, 4, axis=0)
    rows_up = lax.dynamic_slice_in_dim(w_up, device * 4, 4, axis=0)
    gains = lax.dynamic_slice_in_dim(norm_gains, device * 4, 4, axis=1)

    normed, packed = call(
        project_kernel,
        [((2, HALF, D), BF16), ((HEADS, HALF, 384), BF16)],
        [VMEM] * 4,
        vmem=12,
        cost=8_000_000,
    )(low, up, gains_near, w_qkv_near)
    heads = lax.all_to_all(packed, LON, 0, 0, tiled=True).reshape(ROWS, 384)
    heads, scal, rows_qkv, rows_up, gains = lax.optimization_barrier(
        (heads, scal, rows_qkv, rows_up, gains)
    )
    heads, normed = lax.optimization_barrier((heads, normed))
    normed_all = lax.all_gather(normed, LON, axis=0, tiled=False)

    wide = 2 * ROWS
    att, inv = call(
        attend_kernel,
        [((ROWS, 128), BF16), ((ROWS, 128), F32)],
        [SMEM, VMEM],
        [
            pltpu.VMEM((wide, 128), BF16),
            pltpu.VMEM((wide, 128), BF16),
            pltpu.VMEM((2, wide, 128), BF16),
        ],
        vmem=20,
        cost=20_000_000,
    )(scal, heads)
    att_rows = lax.all_to_all(att.reshape(HEADS, HALF, 128), LON, 0, 0, tiled=True)

    out_low, out_up, packed_grad, grad_mixed, sent, keep = call(
        middle_kernel,
        [
            half,
            half,
            ((HEADS, HALF, 128), BF16),
            ((OWN, D), F32),
            ((OWN, 9 * D), BF16),
            ((OWN, 3 * D), BF16),
        ],
        [SMEM] + [VMEM] * 7,
        vmem=24,
    )(core, att_rows, low, up, gains_near, w_out, w_up, w_down)
    grad_heads = lax.all_to_all(packed_grad, LON, 0, 0, tiled=True).reshape(ROWS, 128)
    received = lax.ppermute(sent, "c", across)
    out_back = lax.ppermute(out_low, LAT, backward)
    (pair,) = call(partial_kernel, [((8, 32, 9 * D), BF16)], [VMEM] * 3, vmem=24)(
        keep, sent, received
    )
    part = lax.psum_scatter(pair, "x", scatter_dimension=0, tiled=True)

    block = ((8, 32, 192), BF16)
    (packed_back,) = call(
        attend_back_kernel,
        [((ROWS, 384), BF16)],
        [SMEM] + [VMEM] * 4,
        [
            pltpu.VMEM((wide, 128), BF16),
            pltpu.VMEM((wide, 128), BF16),
            pltpu.VMEM((2, wide, 128), BF16),
            pltpu.VMEM((2, wide, 128), BF16),
            pltpu.VMEM((2, wide, 128), BF16),
        ],
        vmem=32,
        cost=1_000_000_000,
    )(scal, heads, grad_heads, att, inv)
    packed_back, out_back = lax.optimization_barrier((packed_back, out_back))
    grad_packed = lax.all_to_all(
        packed_back.reshape(HEADS, HALF, 384), LON, 0, 0, tiled=True
    )
    mine, other = call(weight_kernel, [block] * 2, [SMEM] + [VMEM] * 2)(
        core, packed_back, normed_all
    )
    theirs = lax.ppermute(other, "c", across)
    blocks = call(pair_kernel, [((2, 32, 192), BF16)] * 4, [SMEM, VMEM, VMEM])(
        x_index, mine, theirs
    )
    blocks = [blocks[0]] + [
        lax.ppermute(blocks[k], "x", [(i, (i + k) % 4) for i in range(4)]) for k in (1, 2, 3)
    ]
    grad_low, grad_up = call(
        input_grad_kernel,
        [half] * 2,
        [VMEM] * 6,
        vmem=12,
    )(grad_packed, low, up, gains_near, grad_mixed, w_qkv_near)

    grad_back = lax.ppermute(grad_low, LAT, backward)
    (joined,) = call(join_kernel, [((16, 4, 9 * D + 256), BF16)], [VMEM] * 5)(part, *blocks)
    got = lax.all_to_all(joined, ("zh",) + LON, 0, 0, tiled=True)
    grad_qkv, grad_out, grad_up_w, grad_down, grad_gains = call(
        last_kernel,
        [
            ((4, 3 * D), F32),
            ((4, D), F32),
            ((4, FF), F32),
            ((16, D), F32),
            ((2, 4), F32),
        ],
        [VMEM] * 4,
    )(got, rows_qkv, rows_up, gains)

    def place(own, moved):
        shape = (3, 2, 16, D)
        return jnp.concatenate([own.reshape(shape), moved.reshape(shape)], axis=1)

    return (
        place(out_up, out_back),
        place(grad_up, grad_back),
        grad_qkv,
        grad_out,
        grad_up_w,
        grad_down,
        grad_gains,
    )


def solution(mesh):
    fine = Mesh(mesh.devices.reshape(AXIS_SIZES), ALL)
    grid = P(None, LAT, LON, None)
    in_specs = (grid, P(LAT, LON), P(), P(), P(), P(), P(), P(), P(), grid)
    rows = P(ALL, None)
    out_specs = (grid, grid, rows, rows, rows, rows, P(None, ALL))
    return jax.shard_map(shards, mesh=fine, in_specs=in_specs, out_specs=out_specs, check_vma=False)
```

```python
import math

import jax
import jax.numpy as jnp
from jax import lax
from jax.experimental import pallas as pl
from jax.experimental.pallas import tpu as pltpu
from jax.sharding import Mesh
from jax.sharding import PartitionSpec as P

LAT = ("x", "zh", "c")
LON = ("zl", "y")
ALL = LAT + LON
AXIS_SIZES = (4, 2, 2, 2, 4)

HEADS = 8
HEAD = 64
D = 512
FF = 2048
HALF = 96
ROWS = 768
OWN = 2 * HALF
QT = 256

F32 = jnp.float32
BF16 = jnp.bfloat16
NT = (((1,), (1,)), ((), ()))
TN = (((0,), (0,)), ((), ()))


def dot(a, b):
    return jnp.dot(a, b, preferred_element_type=F32)


def dot_nt(a, b):
    return lax.dot_general(a, b, NT, preferred_element_type=F32)


def dot_tn(a, b):
    return lax.dot_general(a, b, TN, preferred_element_type=F32)


def norm_stats(values):
    centred = values - jnp.mean(values, axis=-1, keepdims=True)
    variance = jnp.mean(centred * centred, axis=-1, keepdims=True)
    inverse = lax.rsqrt(variance + 1e-05)
    return centred * inverse, inverse


def norm_back(grad, unit, inverse, gain):
    scaled = grad * gain
    first = jnp.mean(scaled, axis=-1, keepdims=True)
    second = jnp.mean(scaled * unit, axis=-1, keepdims=True)
    return inverse * (scaled - first - unit * second)


def swap(pair):
    return pltpu.roll(pair, HEAD, axis=1)


def is_left(rows):
    return lax.broadcasted_iota(jnp.int32, (rows, 2 * HEAD), 1) < HEAD


def pair_sum(values):
    row = lax.broadcasted_iota(jnp.int32, (4 * HEAD, 2 * HEAD), 0) >> 6
    column = lax.broadcasted_iota(jnp.int32, (4 * HEAD, 2 * HEAD), 1) >> 6
    ones = jnp.where((row & 1) == column, 1.0, 0.0).astype(BF16)
    high = values.astype(BF16)
    low = (values - high.astype(F32)).astype(BF16)
    return dot(jnp.concatenate([high, low], axis=1), ones)


def unit_pair(x_ref, offset):
    values = x_ref[:, offset : offset + 2 * HEAD].astype(F32)
    inverse = lax.rsqrt(pair_sum(values * values) + 1e-06)
    return values * inverse, inverse


def unit_back(grad, unit, inverse):
    return inverse * (grad - unit * pair_sum(grad * unit))


def spread(pair):
    swapped = swap(pair)
    left = is_left(ROWS)
    return jnp.where(left, pair, swapped), jnp.where(left, swapped, pair)


def put_spread(ref, pair):
    zero, one = spread(pair)
    ref[:ROWS] = zero.astype(BF16)
    ref[ROWS:] = one.astype(BF16)


def pack_head(array, column):
    cols = slice(column, column + HEAD)
    return [array[:HALF, cols], array[HALF:, cols]]


def unpack_heads(ref, lane):
    return jnp.concatenate([ref[h, :, lane : lane + HEAD] for h in range(HEADS)], axis=1)


def project_kernel(low_ref, up_ref, gain_ref, w_ref, normed_ref, packed_ref):
    hidden = jnp.concatenate([low_ref[:HALF], up_ref[:HALF]], axis=0).astype(F32)
    unit, _ = norm_stats(hidden)
    normed = (unit * gain_ref[0:1, :]).astype(BF16)
    normed_ref[0] = normed[:HALF]
    normed_ref[1] = normed[HALF:]
    projected = dot(normed, w_ref[...]).astype(BF16)
    for h in range(HEADS):
        pieces = []
        for part in range(3):
            pieces += pack_head(projected, part * D + h * HEAD)
        packed_ref[h] = jnp.concatenate(pieces, axis=1)


def value_rows(x_ref):
    values = x_ref[:, 4 * HEAD :].astype(F32)
    swapped = swap(values)
    left = is_left(ROWS)
    return [
        [jnp.where(left, values, 1.0), jnp.where(left, swapped, 1.0)],
        [jnp.where(left, 1.0, swapped), jnp.where(left, 1.0, values)],
    ]


def attend_kernel(scal_ref, x_ref, att_ref, inv_ref, q_s, k_s, v_s):
    factor = scal_ref[0]
    other = scal_ref[2]
    put_spread(q_s, unit_pair(x_ref, 0)[0])
    put_spread(k_s, unit_pair(x_ref, 2 * HEAD)[0])
    values = value_rows(x_ref)
    for a in range(2):
        for b in range(2):
            block = values[a][b] if a == b else values[a][b] * other
            v_s[a, b * ROWS : (b + 1) * ROWS] = block.astype(BF16)
    left = is_left(QT)
    for t in range(ROWS // QT):
        totals = []
        for a in range(2):
            start = a * ROWS + t * QT
            scores = dot_nt(q_s[start : start + QT], k_s[...])
            totals.append(dot(jnp.exp2(scores * factor).astype(BF16), v_s[a]))
        inverse = 1.0 / swap(jnp.where(left, totals[1], totals[0]))
        rows = slice(t * QT, (t + 1) * QT)
        inv_ref[rows] = inverse
        att_ref[rows] = (jnp.where(left, totals[0], totals[1]) * inverse).astype(BF16)


def attend_back_kernel(
    scal_ref, x_ref, grad_ref, att_ref, inv_ref, out_ref, q_s, k_s, v_s, g_s, gd_s
):
    factor = scal_ref[0]
    scale = scal_ref[1]
    other = scal_ref[2]
    left = is_left(ROWS)
    query_unit, query_inverse = unit_pair(x_ref, 0)
    key_unit, key_inverse = unit_pair(x_ref, 2 * HEAD)
    put_spread(q_s, query_unit)
    key_wide = spread(key_unit)
    k_s[:ROWS] = key_wide[0].astype(BF16)
    k_s[ROWS:] = key_wide[1].astype(BF16)
    values = value_rows(x_ref)
    for a in range(2):
        for b in range(2):
            v_s[a, b * ROWS : (b + 1) * ROWS] = values[a][b].astype(BF16)
    grad = grad_ref[...].astype(F32)
    inverse = inv_ref[...]
    delta = swap(pair_sum(grad * att_ref[...].astype(F32)) * inverse)
    high = delta.astype(BF16).astype(F32)
    grad = grad * inverse
    lanes = lax.broadcasted_iota(jnp.int32, (ROWS, 2 * HEAD), 1) & (HEAD - 1)
    tail = jnp.where(lanes == 0, -high, jnp.where(lanes == 1, high - delta, 0.0))
    grad_rows = [jnp.where(left, grad, tail), jnp.where(left, tail, grad)]
    grad_wide = spread(grad)
    for a in range(2):
        rows = slice(a * ROWS, (a + 1) * ROWS)
        for b in range(2):
            mask = 1.0 if a == b else other
            g_s[b, rows] = (grad_rows[a] * mask).astype(BF16)
            gd_s[b, rows] = (grad_wide[a] * mask).astype(BF16)
    dq = [None, None]
    dk = [None, None]
    dv = [None, None]

    def add(sums, place, term):
        sums[place] = term if sums[place] is None else sums[place] + term

    for b in range(2):
        keys = slice(b * ROWS, (b + 1) * ROWS)
        key = k_s[keys]
        key_flat = key_wide[b].T.astype(BF16)
        for a in range(2):
            rows = slice(a * ROWS, (a + 1) * ROWS)
            query = q_s[rows]
            weights = jnp.exp2(dot_nt(key, query) * factor)
            grad_weights = dot_nt(v_s[a, keys], g_s[b, rows])
            grad_scores = (weights * grad_weights).astype(BF16)
            add(dv, b, dot(weights.astype(BF16), gd_s[b, rows]))
            add(dk, b, dot(grad_scores, query))
            add(dq, a, dot(key_flat, grad_scores))
    dq_pair = jnp.where(left, dq[0].T, dq[1].T) * scale
    dk_pair = jnp.where(left, dk[0], dk[1]) * scale
    out_ref[:, : 2 * HEAD] = unit_back(dq_pair, query_unit, query_inverse).astype(BF16)
    out_ref[:, 2 * HEAD : 4 * HEAD] = unit_back(dk_pair, key_unit, key_inverse).astype(BF16)
    out_ref[:, 4 * HEAD :] = jnp.where(left, dv[0], dv[1]).astype(BF16)


def weight_kernel(core_ref, packed_ref, normed_ref, mine_ref, other_ref):
    product = None
    for a in range(2):
        pieces = []
        for part in range(3):
            start = part * 2 * HEAD + a * HEAD
            pieces.append(packed_ref[:, start : start + HEAD])
        normed = jnp.concatenate([normed_ref[i, a] for i in range(8)], axis=0)
        term = dot_tn(normed, jnp.concatenate(pieces, axis=1))
        product = term if product is None else product + term
    first = core_ref[0] == 0
    for g in range(8):
        zero = product[g * 64 : g * 64 + 32]
        one = product[g * 64 + 32 : g * 64 + 64]
        mine_ref[g] = jnp.where(first, zero, one).astype(BF16)
        other_ref[g] = jnp.where(first, one, zero).astype(BF16)


def pair_kernel(x_ref, mine_ref, theirs_ref, zero_ref, one_ref, two_ref, three_ref):
    for k, ref in enumerate((zero_ref, one_ref, two_ref, three_ref)):
        block = pl.ds(((x_ref[0] + k) & 3) * 2, 2)
        ref[...] = (mine_ref[block].astype(F32) + theirs_ref[block].astype(F32)).astype(BF16)


def join_kernel(part_ref, zero_ref, one_ref, two_ref, three_ref, out_ref):
    for z in range(2):
        narrow = part_ref[z, :, : 5 * D].astype(F32)
        qkv = zero_ref[z].astype(F32)
        for ref in (one_ref, two_ref, three_ref):
            qkv = qkv + ref[z].astype(F32)
        for j in range(8):
            rows = slice(4 * j, 4 * j + 4)
            out_ref[z * 8 + j, :, : 5 * D] = narrow[rows].astype(BF16)
            start = 5 * D + D * (j // 2)
            down = part_ref[z, 16 * (j % 2) : 16 * (j % 2) + 16, start : start + D].astype(F32)
            for s in range(4):
                cols = slice((5 + s) * D, (6 + s) * D)
                out_ref[z * 8 + j, :, cols] = down[4 * s : 4 * s + 4].astype(BF16)
            padded = jnp.concatenate([qkv[rows], jnp.zeros((4, HEAD), F32)], axis=1)
            out_ref[z * 8 + j, :, 9 * D :] = padded.astype(BF16)


def last_kernel(
    got_ref, qkv_rows_ref, up_rows_ref, gains_ref, qkv_ref, out_ref, up_ref, down_ref, gain_ref
):
    grad_scale = 1.0 / math.sqrt(OWN * 128)
    total = got_ref[0, :, : 9 * D].astype(F32)
    for i in range(1, 16):
        total = total + got_ref[i, :, : 9 * D].astype(F32)
    total = total * grad_scale
    out_ref[...] = total[:, :D]
    up = total[:, D : 5 * D]
    up_ref[...] = up
    for s in range(4):
        down_ref[4 * s : 4 * s + 4] = total[:, (5 + s) * D : (6 + s) * D]
    heads = []
    for h in range(HEADS):
        pair = got_ref[h, :, 9 * D :].astype(F32) + got_ref[8 + h, :, 9 * D :].astype(F32)
        heads.append(pair * grad_scale)
    pieces = [heads[h][:, p * HEAD : (p + 1) * HEAD] for p in range(3) for h in range(HEADS)]
    qkv = jnp.concatenate(pieces, axis=1)
    qkv_ref[...] = qkv
    eye = lax.broadcasted_iota(jnp.int32, (4, 4), 0) == lax.broadcasted_iota(
        jnp.int32, (4, 4), 1
    )
    products = (qkv * qkv_rows_ref[...].astype(F32), up * up_rows_ref[...].astype(F32))
    for i, product in enumerate(products):
        column = jnp.sum(product, axis=1, keepdims=True)
        row = jnp.sum(jnp.where(eye, column, 0.0), axis=0, keepdims=True)
        gain_ref[i : i + 1] = row / gains_ref[i : i + 1]


def load_all(pairs, sems):
    loads = [
        pltpu.make_async_copy(source, target, sems.at[i])
        for i, (source, target) in enumerate(pairs)
    ]
    for load in loads:
        load.start()
    return loads


def near_kernel(*refs):
    count = (len(refs) - 1) // 2
    for load in load_all(tuple(zip(refs[:count], refs[count:-1])), refs[-1]):
        load.wait()


def enter_kernel(
    field_hbm, mask_hbm, embed_hbm, cot_hbm, low_ref, up_ref,
    field_ref, mask_ref, embed_ref, cot_ref, sems,
):
    loads = load_all(
        (
            (mask_hbm, mask_ref),
            (embed_hbm, embed_ref),
            (field_hbm, field_ref),
            (cot_hbm, cot_ref),
        ),
        sems,
    )
    for load in loads:
        load.wait()
    sea = embed_ref[0:1].astype(F32)
    land = embed_ref[1:2].astype(F32)
    mask = (mask_ref[...] == 1).astype(F32)
    eye = lax.broadcasted_iota(jnp.int32, (16, 16), 0) == lax.broadcasted_iota(
        jnp.int32, (16, 16), 1
    )
    for row in range(4):
        column = jnp.sum(jnp.where(eye, mask[row : row + 1], 0.0), axis=1, keepdims=True)
        chosen = jnp.where(column > 0.5, land, sea)
        ref = up_ref if row < 2 else low_ref
        for level in range(3):
            start = (level * 2 + row % 2) * 16
            rows = slice(start, start + 16)
            ref[rows] = (field_ref[level, row].astype(F32) + chosen).astype(BF16)
            ref[HALF + start : HALF + start + 16] = cot_ref[level, row]


def core_columns(array, width, core):
    pieces = [
        array[:, (2 * g + core) * width : (2 * g + core + 1) * width] for g in range(8)
    ]
    return jnp.concatenate(pieces, axis=1)


def middle_kernel(
    core_ref, att_ref, low_ref, up_ref, gain_ref, w_out_ref, w_up_ref, w_down_ref,
    out_low_ref, out_up_ref, packed_ref, gm_ref, send_ref, keep_ref,
):
    first = core_ref[0] == 0
    attended = jnp.concatenate([unpack_heads(att_ref, 0), unpack_heads(att_ref, HEAD)], axis=0)
    hidden = jnp.concatenate([low_ref[:HALF], up_ref[:HALF]], axis=0).astype(F32)
    cot = jnp.concatenate([low_ref[HALF:], up_ref[HALF:]], axis=0)
    gain = gain_ref[1:2, :]
    mixed = (hidden + dot(attended, w_out_ref[...])).astype(BF16).astype(F32)
    unit, inverse = norm_stats(mixed)
    normed = (unit * gain).astype(BF16)
    pre = dot(normed, w_up_ref[...])
    root = math.sqrt(2.0 / math.pi)
    square = pre * pre
    bend = jnp.tanh(root * pre * (1.0 + 0.044715 * square))
    half_up = 0.5 * (1.0 + bend)
    activated = (pre * half_up).astype(BF16)
    slope = half_up + 0.5 * pre * (1.0 - bend * bend) * root * (1.0 + 3 * 0.044715 * square)
    grad_pre = (dot_nt(cot, w_down_ref[...]) * slope).astype(BF16)
    grad_normed = dot_nt(grad_pre, w_up_ref[...])
    grad_mixed = cot.astype(F32) + norm_back(grad_normed, unit, inverse, gain)
    gm_ref[...] = grad_mixed
    grad_low = grad_mixed.astype(BF16)
    grad_attended = dot_nt(grad_low, w_out_ref[...]).astype(BF16)
    for h in range(HEADS):
        packed_ref[h] = jnp.concatenate(pack_head(grad_attended, h * HEAD), axis=1)
    layer_out = (mixed + dot(activated, w_down_ref[...])).astype(BF16)
    out_low_ref[...] = layer_out[:HALF]
    out_up_ref[...] = layer_out[HALF:]
    start = 0
    for array, width in ((activated, 128), (normed, 32), (attended, 32)):
        zero = core_columns(array, width, 0)
        one = core_columns(array, width, 1)
        cols = slice(start, start + 8 * width)
        keep_ref[:, cols] = jnp.where(first, zero, one)
        send_ref[:, cols] = jnp.where(first, one, zero)
        start += 8 * width
    for array in (cot, grad_pre, grad_low):
        send_ref[:, start : start + array.shape[1]] = array
        start += array.shape[1]


def partial_kernel(keep_ref, sent_ref, got_ref, out_ref):
    def both(own_ref, start, width):
        cols = slice(start, start + width)
        return jnp.concatenate([own_ref[:, cols], got_ref[:, cols]], axis=0)

    product = dot_tn(both(keep_ref, 0, 2 * D), both(sent_ref, 3 * D, D)).astype(BF16)
    for g in range(8):
        for s in range(4):
            at = g * 128 + s * 32
            out_ref[g, :, (5 + s) * D : (6 + s) * D] = product[at : at + 32]
    product = dot_tn(both(keep_ref, 2 * D, D // 2), both(sent_ref, 4 * D, FF)).astype(BF16)
    for g in range(8):
        out_ref[g, :, D : 5 * D] = product[g * 32 : g * 32 + 32]
    product = dot_tn(both(keep_ref, 5 * D // 2, D // 2), both(sent_ref, 8 * D, D)).astype(BF16)
    for g in range(8):
        out_ref[g, :, :D] = product[g * 32 : g * 32 + 32]


def input_grad_kernel(
    packed_ref, low_ref, up_ref, gain_ref, gm_ref, w_ref, glow_ref, gup_ref
):
    halves = []
    for a in range(2):
        parts = [unpack_heads(packed_ref, place * 128 + a * HEAD) for place in range(3)]
        halves.append(jnp.concatenate(parts, axis=1))
    grad_projected = jnp.concatenate(halves, axis=0)
    hidden = jnp.concatenate([low_ref[:HALF], up_ref[:HALF]], axis=0).astype(F32)
    unit, inverse = norm_stats(hidden)
    grad_normed = dot_nt(grad_projected, w_ref[...])
    grad = gm_ref[...] + norm_back(grad_normed, unit, inverse, gain_ref[0:1, :])
    grad = grad.astype(BF16)
    glow_ref[...] = grad[:HALF]
    gup_ref[...] = grad[HALF:]


VMEM = pl.BlockSpec(memory_space=pltpu.VMEM)
SMEM = pl.BlockSpec(memory_space=pltpu.SMEM)
ANY = pl.BlockSpec(memory_space=pl.ANY)


def call(kernel, outs, specs, scratch=(), vmem=12, cost=3_000_000):
    shapes = tuple(jax.ShapeDtypeStruct(shape, dtype) for shape, dtype in outs)
    return pl.pallas_call(
        kernel,
        out_shape=shapes,
        in_specs=specs,
        out_specs=(VMEM,) * len(outs),
        scratch_shapes=list(scratch),
        compiler_params=pltpu.CompilerParams(vmem_limit_bytes=vmem * 1024 * 1024),
        cost_estimate=pl.CostEstimate(flops=0, bytes_accessed=cost, transcendentals=0),
    )


def shards(
    fields, land_sea, surface_embed, norm_gains, w_qkv, head_scales, w_out, w_up, w_down, cotangent
):
    lat = lax.axis_index(LAT)
    lon = lax.axis_index(LON)
    device = lax.axis_index(ALL)
    core = lax.axis_index("c").astype(jnp.int32).reshape(1)
    x_index = lax.axis_index("x").astype(jnp.int32).reshape(1)
    forward = [(i, (i + 1) % 16) for i in range(16)]
    backward = [(j, i) for i, j in forward]
    across = [(0, 1), (1, 0)]
    half = ((HALF, D), BF16)
    low, up = call(
        enter_kernel,
        [((OWN, D), BF16)] * 2,
        [ANY] * 4,
        [
            pltpu.VMEM((3, 4, 16, D), BF16),
            pltpu.VMEM((4, 16), jnp.int32),
            pltpu.VMEM((2, D), BF16),
            pltpu.VMEM((3, 4, 16, D), BF16),
            pltpu.SemaphoreType.DMA((4,)),
        ],
        vmem=60,
    )(fields, land_sea, surface_embed, cotangent)
    low = lax.ppermute(low, LAT, forward)
    w_qkv_near, gains_near = call(
        near_kernel,
        [((D, 3 * D), BF16), ((2, D), F32)],
        [ANY] * 2,
        [pltpu.SemaphoreType.DMA((2,))],
    )(w_qkv, norm_gains)
    low, w_qkv_near, gains_near = lax.optimization_barrier((low, w_qkv_near, gains_near))

    scale = head_scales[lon]
    valid = jnp.where(lat == 0, 0.0, 1.0)
    scal = jnp.stack([scale * (0.5 * math.log2(math.e)), scale, valid]).astype(F32)
    rows_qkv = lax.dynamic_slice_in_dim(w_qkv, device * 4, 4, axis=0)
    rows_up = lax.dynamic_slice_in_dim(w_up, device * 4, 4, axis=0)
    gains = lax.dynamic_slice_in_dim(norm_gains, device * 4, 4, axis=1)

    normed, packed = call(
        project_kernel,
        [((2, HALF, D), BF16), ((HEADS, HALF, 384), BF16)],
        [VMEM] * 4,
        vmem=12,
        cost=8_000_000,
    )(low, up, gains_near, w_qkv_near)
    heads = lax.all_to_all(packed, LON, 0, 0, tiled=True).reshape(ROWS, 384)
    heads, scal, rows_qkv, rows_up, gains = lax.optimization_barrier(
        (heads, scal, rows_qkv, rows_up, gains)
    )
    wide = 2 * ROWS
    att, inv = call(
        attend_kernel,
        [((ROWS, 128), BF16), ((ROWS, 128), F32)],
        [SMEM, VMEM],
        [
            pltpu.VMEM((wide, 128), BF16),
            pltpu.VMEM((wide, 128), BF16),
            pltpu.VMEM((2, wide, 128), BF16),
        ],
        vmem=20,
        cost=20_000_000,
    )(scal, heads)
    att, normed = lax.optimization_barrier((att, normed))
    normed_all = lax.all_gather(normed, LON, axis=0, tiled=False)
    att_rows = lax.all_to_all(att.reshape(HEADS, HALF, 128), LON, 0, 0, tiled=True)

    out_low, out_up, packed_grad, grad_mixed, sent, keep = call(
        middle_kernel,
        [
            half,
            half,
            ((HEADS, HALF, 128), BF16),
            ((OWN, D), F32),
            ((OWN, 9 * D), BF16),
            ((OWN, 3 * D), BF16),
        ],
        [SMEM] + [VMEM] * 7,
        vmem=24,
    )(core, att_rows, low, up, gains_near, w_out, w_up, w_down)
    grad_heads = lax.all_to_all(packed_grad, LON, 0, 0, tiled=True).reshape(ROWS, 128)
    received = lax.ppermute(sent, "c", across)
    out_back = lax.ppermute(out_low, LAT, backward)
    (pair,) = call(partial_kernel, [((8, 32, 9 * D), BF16)], [VMEM] * 3, vmem=24)(
        keep, sent, received
    )
    part = lax.psum_scatter(pair, "x", scatter_dimension=0, tiled=True)

    block = ((8, 32, 192), BF16)
    (packed_back,) = call(
        attend_back_kernel,
        [((ROWS, 384), BF16)],
        [SMEM] + [VMEM] * 4,
        [
            pltpu.VMEM((wide, 128), BF16),
            pltpu.VMEM((wide, 128), BF16),
            pltpu.VMEM((2, wide, 128), BF16),
            pltpu.VMEM((2, wide, 128), BF16),
            pltpu.VMEM((2, wide, 128), BF16),
        ],
        vmem=32,
        cost=1_000_000_000,
    )(scal, heads, grad_heads, att, inv)
    packed_back, out_back = lax.optimization_barrier((packed_back, out_back))
    grad_packed = lax.all_to_all(
        packed_back.reshape(HEADS, HALF, 384), LON, 0, 0, tiled=True
    )
    mine, other = call(weight_kernel, [block] * 2, [SMEM] + [VMEM] * 2)(
        core, packed_back, normed_all
    )
    theirs = lax.ppermute(other, "c", across)
    blocks = call(pair_kernel, [((2, 32, 192), BF16)] * 4, [SMEM, VMEM, VMEM])(
        x_index, mine, theirs
    )
    blocks = [blocks[0]] + [
        lax.ppermute(blocks[k], "x", [(i, (i + k) % 4) for i in range(4)]) for k in (1, 2, 3)
    ]
    grad_low, grad_up = call(
        input_grad_kernel,
        [half] * 2,
        [VMEM] * 6,
        vmem=12,
    )(grad_packed, low, up, gains_near, grad_mixed, w_qkv_near)

    grad_back = lax.ppermute(grad_low, LAT, backward)
    (joined,) = call(join_kernel, [((16, 4, 9 * D + 256), BF16)], [VMEM] * 5)(part, *blocks)
    got = lax.all_to_all(joined, ("zh",) + LON, 0, 0, tiled=True)
    grad_qkv, grad_out, grad_up_w, grad_down, grad_gains = call(
        last_kernel,
        [
            ((4, 3 * D), F32),
            ((4, D), F32),
            ((4, FF), F32),
            ((16, D), F32),
            ((2, 4), F32),
        ],
        [VMEM] * 4,
    )(got, rows_qkv, rows_up, gains)

    def place(own, moved):
        shape = (3, 2, 16, D)
        return jnp.concatenate([own.reshape(shape), moved.reshape(shape)], axis=1)

    return (
        place(out_up, out_back),
        place(grad_up, grad_back),
        grad_qkv,
        grad_out,
        grad_up_w,
        grad_down,
        grad_gains,
    )


def solution(mesh):
    fine = Mesh(mesh.devices.reshape(AXIS_SIZES), ALL)
    grid = P(None, LAT, LON, None)
    in_specs = (grid, P(LAT, LON), P(), P(), P(), P(), P(), P(), P(), grid)
    rows = P(ALL, None)
    out_specs = (grid, grid, rows, rows, rows, rows, P(None, ALL))
    return jax.shard_map(shards, mesh=fine, in_specs=in_specs, out_specs=out_specs, check_vma=False)
```
